32 devices in a mesh: tm: 8 (over z, x), item: 4 (over y, core).
Axes of the slice: x: 2, y: 2, z: 4, core: 2. Of those that a mesh axis runs over, the one named last changes fastest.
Arguments:
- inputs: float32 [32, 8192, 128], P('item', 'tm'), may hold values from -16 to 16
- lengths: int32 [32], P('item'), may hold values from 4096 to 8192, as said below
- counts: int32 [32], P('item'), may hold values from 2 to 3, as said below
- weight_in: float32 [128, 512], replicated, may hold values from -0.5 to 0.5
- bias_in: float32 [512], replicated, may hold values from -1.75 to 1.75
- slope_in: float32 [512], replicated, may hold values from 0.1 to 0.5
- gain_in: float32 [512], replicated, may hold values from 0.25 to 1.75
- shift_in: float32 [512], replicated, may hold values from -1.75 to 1.75
- channelwise_taps: float32 [3, 512], replicated, may hold values from -3.5 to 3.5
- channelwise_bias: float32 [512], replicated, may hold values from -1.75 to 1.75
- slope_out: float32 [512], replicated, may hold values from 0.1 to 0.5
- gain_out: float32 [512], replicated, may hold values from 0.25 to 1.75
- shift_out: float32 [512], replicated, may hold values from -1.75 to 1.75
- weight_res: float32 [512, 128], replicated, may hold values from -0.25 to 0.25
- bias_res: float32 [128], replicated, may hold values from -1.75 to 1.75
- weight_skip: float32 [512, 128], replicated, may hold values from -0.25 to 0.25
- bias_skip: float32 [128], replicated, may hold values from -1.75 to 1.75
- grad_residual: float32 [32, 8192, 128], P('item', 'tm'), may hold values from -6 to 6
- grad_skip: float32 [32, 3, 8192, 128], P('item', None, 'tm'), may hold values from -3.5 to 3.5
Outputs:
- residual_out: float32 [32, 8192, 128], P('item', 'tm')
- skip_out: float32 [32, 8192, 128], P('item', 'tm')
- grad_inputs: float32 [32, 8192, 128], P('item', 'tm')
- grad_weight_in: float32 [128, 512], replicated
- grad_bias_in: float32 [512], replicated
- grad_slope_in: float32 [512], replicated
- grad_gain_in: float32 [512], replicated
- grad_shift_in: float32 [512], replicated
- grad_depth_taps: float32 [3, 512], replicated
- grad_depth_bias: float32 [512], replicated
- grad_slope_out: float32 [512], replicated
- grad_gain_out: float32 [512], replicated
- grad_shift_out: float32 [512], replicated
- grad_weight_res: float32 [512, 128], replicated
- grad_bias_res: float32 [128], replicated
- grad_weight_skip: float32 [512, 128], replicated
- grad_bias_skip: float32 [128], replicated
The draws below stay inside these ranges and needn't reach their ends.
Inputs may be any that keep to these rules, and one draw needn't show every extreme that they name: `lengths`: among the 8 items of each index of item, one has all 8192 frames valid. `counts`: both values occur in every draw.
All inputs are finite; a program needn't handle non-finite values.
Results may differ from the reference program's by a relative error of at most 0.0003.
Values sent between devices are 32-bit elements; how exact they have to be, the bound alone decides.
No kernel may reach another device: no remote copies, remote signals or barrier semaphores. Data moves between devices by JAX's collectives and lax.ppermute only.
A program may use at most 256 MiB of HBM per device.

```python
import jax
import jax.numpy as jnp
from jax import lax

B = 128
H = 512
TAP_SPACING = 128
SOURCES = 3
ITEMS_DEV = 8
ITEM_FRAMES = 8192
ITEMS = 32


def draw_inputs(key, part):
    key = jax.random.fold_in(key, 11)
    place = jnp.arange(ITEM_FRAMES, dtype=jnp.float32) / ITEM_FRAMES
    base = jnp.clip(jax.random.normal(key, (ITEMS, ITEM_FRAMES, B), jnp.float32), -4.0, 4.0)
    rising = jnp.exp(1.0986 * place)
    return base * rising[None, :, None]


def draw_lengths(key, part):
    key = jax.random.fold_in(key, 12)
    leading_part, second = jax.random.split(key)
    drawn = jax.random.randint(leading_part, (ITEMS,), ITEM_FRAMES // 2, ITEM_FRAMES + 1)
    chosen = jax.random.randint(second, (ITEMS // ITEMS_DEV,), 0, ITEMS_DEV)
    index = jnp.arange(ITEMS, dtype=jnp.int32)
    return jnp.where(index % ITEMS_DEV == chosen[index // ITEMS_DEV], ITEM_FRAMES, drawn).astype(jnp.int32)


def draw_counts(key, part):
    key = jax.random.fold_in(key, 13)
    leading_part, second = jax.random.split(key)
    drawn = jax.random.randint(leading_part, (ITEMS,), 2, 4)
    place = jax.random.randint(second, (), 0, ITEMS)
    index = jnp.arange(ITEMS, dtype=jnp.int32)
    drawn = jnp.where(index == place, 2, drawn)
    drawn = jnp.where(index == (place + 1) % ITEMS, 3, drawn)
    return drawn.astype(jnp.int32)


def level_of(rng, dims, pieces, least, largest):
    def one(position, parts):
        heights = jax.random.uniform(jax.random.fold_in(jax.random.fold_in(rng, 6), position), (parts,), jnp.float32, least / len(pieces), largest / len(pieces))
        return jnp.repeat(jnp.exp(heights), dims[position] // parts).reshape((-1,) + (1,) * (len(dims) - position - 1))

    loudness = one(*pieces[0])
    for cut in pieces[1:]:
        loudness = loudness * one(*cut)
    return loudness


def noise(rng, dims, deviation, limit, pieces=(), held_as=jnp.bfloat16):
    values = jax.random.normal(rng, dims, jnp.float32) * deviation
    if len(pieces) > 0:
        values = level_of(rng, dims, pieces, -0.22, 0.18) * values
    return jnp.clip(values, min=-limit, max=limit).astype(held_as)


def setup_inputs(seed: int = 0) -> dict:
    splits = jax.random.split(jax.random.key(seed), 20)
    return {
        "inputs": draw_inputs(jax.random.fold_in(splits[19], 71), 0),
        "lengths": draw_lengths(jax.random.fold_in(splits[19], 71), 0),
        "counts": draw_counts(jax.random.fold_in(splits[19], 71), 0),
        "weight_in": noise(splits[3], (B, H), B ** -0.5, 0.5, (), jnp.float32),
        "bias_in": noise(splits[4], (H,), 0.3, 1.75, (), jnp.float32),
        "slope_in": jnp.clip(jax.random.uniform(splits[5], (H,), jnp.float32, 0.1, 0.5), 0.1, 0.5),
        "gain_in": jnp.clip(1.0 + 0.15 * jax.random.normal(splits[6], (H,), jnp.float32), 0.25, 1.75),
        "shift_in": noise(splits[7], (H,), 0.3, 1.75, (), jnp.float32),
        "channelwise_taps": noise(splits[8], (3, H), 3 ** -0.5, 3.5, (), jnp.float32),
        "channelwise_bias": noise(splits[9], (H,), 0.3, 1.75, (), jnp.float32),
        "slope_out": jnp.clip(jax.random.uniform(splits[10], (H,), jnp.float32, 0.1, 0.5), 0.1, 0.5),
        "gain_out": jnp.clip(1.0 + 0.15 * jax.random.normal(splits[11], (H,), jnp.float32), 0.25, 1.75),
        "shift_out": noise(splits[12], (H,), 0.3, 1.75, (), jnp.float32),
        "weight_res": noise(splits[13], (H, B), H ** -0.5, 0.25, (), jnp.float32),
        "bias_res": noise(splits[14], (B,), 0.3, 1.75, (), jnp.float32),
        "weight_skip": noise(splits[15], (H, B), H ** -0.5, 0.25, (), jnp.float32),
        "bias_skip": noise(splits[16], (B,), 0.3, 1.75, (), jnp.float32),
        "grad_residual": noise(splits[17], (ITEMS, ITEM_FRAMES, B), 1.0, 6.0, ((0, 4), (1, 8)), jnp.float32),
        "grad_skip": noise(splits[18], (ITEMS, SOURCES, ITEM_FRAMES, B), 0.6, 3.5, ((0, 4), (2, 8)), jnp.float32),
    }


epsilon = 1e-05
highest = lax.Precision.HIGHEST

@jax.custom_vjp
def low(v):
    return lax.optimization_barrier(v.astype(jnp.bfloat16)).astype(jnp.float32)

@jax.custom_vjp
def low_back(v):
    return v

def low_keep(v):
    return (low(v), None)

def low_pass(kept, grad):
    return (grad,)

def back_keep(v):
    return (v, None)

def back_low(kept, grad):
    return (low(grad),)
low.defvjp(low_keep, low_pass)
low_back.defvjp(back_keep, back_low)

def soft_prelu(value, slope):
    return jax.nn.softplus(value) - slope * jax.nn.softplus(-value)

def global_norm(value, mask, count, gain, shift):
    mean = jnp.sum(value * mask) / count
    centered = (value - mean) * mask
    variance = jnp.sum(centered * centered) / count
    normal = (value - mean) * lax.rsqrt(variance + epsilon)
    return (gain * normal + shift) * mask

def block_item(params, sample, mask):
    weight_in, bias_in, slope_in, gain_in, shift_in, channelwise_taps, channelwise_bias, slope_out, gain_out, shift_out, weight_res, bias_res, weight_skip, bias_skip = params
    count = jnp.sum(mask) * weight_in.shape[1]
    hidden = jnp.dot(sample, weight_in, precision=highest, preferred_element_type=jnp.float32) + bias_in
    leading_part = global_norm(soft_prelu(hidden, slope_in), mask, count, gain_in, shift_in)
    extended_hidden = jnp.pad(leading_part, ((TAP_SPACING, TAP_SPACING), (0, 0)))
    convolved_hidden = channelwise_taps[0] * extended_hidden[:ITEM_FRAMES] + channelwise_taps[1] * leading_part + channelwise_taps[2] * extended_hidden[2 * TAP_SPACING:] + channelwise_bias
    second = global_norm(soft_prelu(convolved_hidden, slope_out), mask, count, gain_out, shift_out)
    residual = sample + jnp.dot(second, weight_res, precision=highest, preferred_element_type=jnp.float32) + bias_res
    skip = jnp.dot(second, weight_skip, precision=highest, preferred_element_type=jnp.float32) + bias_skip
    return (residual, skip)

def reference(inputs, lengths, counts, weight_in, bias_in, slope_in, gain_in, shift_in, channelwise_taps, channelwise_bias, slope_out, gain_out, shift_out, weight_res, bias_res, weight_skip, bias_skip, grad_residual, grad_skip):
    params = (weight_in, bias_in, slope_in, gain_in, shift_in, channelwise_taps, channelwise_bias, slope_out, gain_out, shift_out, weight_res, bias_res, weight_skip, bias_skip)
    zeros = jax.tree.map(jnp.zeros_like, params)

    def one_item(carry, item):
        sample, length, sources, cot_res, cot_skip = item
        mask = (jnp.arange(ITEM_FRAMES, dtype=jnp.int32) < length).astype(jnp.float32)[:, None]
        alive = (jnp.arange(SOURCES, dtype=jnp.int32) < sources).astype(jnp.float32)
        skip_cot = lax.optimization_barrier(jnp.sum(cot_skip * alive[:, None, None], axis=0))
        outputs, pullback = jax.vjp(lambda values, data: block_item(values, data, mask), params, sample)
        grads, grad_sample = pullback((cot_res, skip_cot))
        carry = jax.tree.map(jnp.add, carry, grads)
        return (carry, (outputs[0], outputs[1], grad_sample))
    totals, (residual, skip, grad_inputs) = lax.scan(one_item, zeros, (inputs, lengths, counts, grad_residual, grad_skip))
    return (residual, skip, grad_inputs, totals[0], totals[1], totals[2], totals[3], totals[4], totals[5], totals[6], totals[7], totals[8], totals[9], totals[10], totals[11], totals[12], totals[13])
```

```python
import functools

import jax
import jax.numpy as jnp
from jax import lax
from jax.experimental import pallas as pl
from jax.experimental.pallas import tpu as pltpu
from jax.sharding import PartitionSpec as P

TAP = 128
LANES = 128
EPSILON = 1e-05
LN2 = 0.6931471805599453
LOG2E = 1.4426950408889634
VMEM = 58 * 2**20
f32 = jnp.float32
bf16 = jnp.bfloat16

BIAS_IN, SLOPE_IN, GAIN_IN, SHIFT_IN, TAP0, TAP1, TAP2, BIAS_DW, SLOPE_OUT, GAIN_OUT, SHIFT_OUT = range(11)
(R_P, R_S, R_SS, R_GD, R_GS, R_H0, R_H1, R_H2, R_HF0, R_HF1, R_HF2, R_PF0, R_PF1, R_PF2,
 R_A0, R_A1, R_A2, R_Z0, R_Z1, R_Z2, R_GM) = range(21)
ROWS = 24


def split(x):
    hi = x.astype(bf16)
    lo = (x - hi.astype(f32)).astype(bf16)
    return hi, lo


def dot(a, b):
    return jnp.dot(a, b, preferred_element_type=f32)


def dot0(a, b):
    return lax.dot_general(a, b, (((0,), (0,)), ((), ())), preferred_element_type=f32)


def product3(x, w3):
    hi, lo = split(x)
    return dot(jnp.concatenate([hi, hi, lo], axis=1), w3)


def stacked3(w):
    hi, lo = split(w)
    return jnp.concatenate([hi, lo, hi], axis=0)


def act(v, a, c):
    e = jnp.exp2(-LOG2E * jnp.abs(v))
    return jnp.maximum(v, a * v) + c * jnp.log2(1.0 + e)


def fold(x):
    rows, cols = x.shape
    return x.reshape(rows // 8, 8, cols).sum(axis=0)


def mask_rows(first, rows, length):
    row = lax.broadcasted_iota(jnp.int32, (rows, 1), 0) + first
    return ((row >= 0) & (row < length)).astype(f32)


def lane_put(values):
    shape = values[0].shape[:-1] + (LANES,)
    lane = lax.broadcasted_iota(jnp.int32, shape, len(shape) - 1)
    out = jnp.zeros(shape, f32)
    for k, v in enumerate(values):
        out = jnp.where(lane == k, jnp.broadcast_to(v, shape), out)
    return out


def first_kernel(rows, len_ref, tm_ref, x_ref, w_ref, pc_ref, v_ref, st_ref, w3):
    i = pl.program_id(0)
    frames, width = v_ref.shape[1:]

    @pl.when(i == 0)
    def _():
        w3[...] = stacked3(w_ref[...])

    length = len_ref[i]
    start = tm_ref[0] * frames
    b, a = pc_ref[BIAS_IN : BIAS_IN + 1], pc_ref[SLOPE_IN : SLOPE_IN + 1]
    c = (1.0 - a) * LN2

    def chunk(k, carry):
        total, square, centre = carry
        r0 = pl.multiple_of(k * rows, rows)
        h = product3(x_ref[0, pl.ds(r0, rows), :], w3[...]) + b
        v = act(h, a, c)
        v_ref[0, pl.ds(r0, rows), :] = v
        centre = jnp.where(k == 0, jnp.broadcast_to(v[0:1], (8, width)), centre)
        m = mask_rows(start + r0, rows, length)
        d = v.reshape(rows // 8, 8, width) - centre[None]
        dm = d * m.reshape(rows // 8, 8, 1)
        return total + dm.sum(axis=0), square + (dm * d).sum(axis=0), centre

    zero = jnp.zeros((8, width), f32)
    total, square, centre = lax.fori_loop(0, frames // rows, chunk, (zero, zero, zero))
    n = jnp.clip(length - start, 0, frames).astype(f32)
    safe = jnp.maximum(jnp.full((1, 1), n, f32), 1.0)
    total = total.sum(axis=0, keepdims=True) / safe
    square = square.sum(axis=0, keepdims=True)
    channel = centre[0:1] + total
    mean = channel.sum(axis=1, keepdims=True) / width
    dev = channel - mean
    spread = (square - safe * total * total + safe * dev * dev).sum(axis=1, keepdims=True)
    some = (n > 0).astype(f32)
    row = lane_put([mean * some, spread * some, jnp.full((1, 1), n, f32)])
    st_ref[:, pl.ds(i, 1), :] = jnp.broadcast_to(row[None], (st_ref.shape[0], 1, LANES))


def merged(gathered, width):
    mean_d, spread_d, n_d = gathered[:, :, 0:1], gathered[:, :, 1:2], gathered[:, :, 2:3]
    n = n_d.sum(axis=0)
    mean = (n_d * mean_d).sum(axis=0) / n
    dev = mean_d - mean[None]
    spread = (spread_d + n_d * width * dev * dev).sum(axis=0)
    count = n * width
    return mean, lax.rsqrt(spread / count + EPSILON), count


def wide(x, width):
    return jnp.broadcast_to(x[:, 0:1], (x.shape[0], width))


def second_kernel(
    rows, len_ref, cnt_ref, tm_ref, v_ref, xb_ref, xa_ref, gr_ref, gk_ref, w_ref, wr_ref, ws_ref, pc_ref, ga_ref,
    f0_ref, f1_ref, f2_ref, z_ref, y_ref, ch_ref, st_ref, bias_ref,
    w3, wt3, wg3, stat, fst, grc, gsc, acc, yacc,
):
    i = pl.program_id(0)
    frames, width = v_ref.shape[1:]
    base = gr_ref.shape[2]
    total_frames = frames * ga_ref.shape[0]

    def par(k):
        return pc_ref[k : k + 1]

    @pl.when(i == 0)
    def _():
        w3[...] = stacked3(w_ref[...])
        both = jnp.concatenate([wr_ref[...], ws_ref[...]], axis=1)
        wt3[...] = stacked3(both.T)
        gain = pc_ref[GAIN_OUT : GAIN_OUT + 1]
        scaled = jnp.concatenate([(wr_ref[...].T * gain).T, (ws_ref[...].T * gain).T], axis=1)
        wg3[...] = stacked3(scaled)
        mean, scale, _ = merged(ga_ref[...], width)
        stat[0] = jnp.broadcast_to(mean, stat.shape[1:])
        stat[1] = jnp.broadcast_to(scale, stat.shape[1:])
        bias_ref[...] = jnp.zeros_like(bias_ref)

    length = len_ref[i]
    start = tm_ref[0] * frames
    mean = wide(stat[0, pl.ds(i, 1), :], width)
    scale = wide(stat[1, pl.ds(i, 1), :], width)
    gain = par(GAIN_IN) * scale
    shift = par(SHIFT_IN) - gain * mean
    a1 = par(SLOPE_IN)
    c1 = (1.0 - a1) * LN2

    for ref, r0 in ((xb_ref, 0), (xa_ref, frames + TAP)):
        h = product3(ref[0], w3[...]) + par(BIAS_IN)
        m = mask_rows(start + r0 - TAP, TAP, length)
        fst[r0 : r0 + TAP, :] = m * (gain * act(h, a1, c1) + shift)

    def lift(k, _):
        r0 = pl.multiple_of(k * rows, rows)
        m = mask_rows(start + r0, rows, length)
        fst[pl.ds(TAP + r0, rows), :] = m * (gain * v_ref[0, pl.ds(r0, rows), :] + shift)
        return 0

    lax.fori_loop(0, frames // rows, lift, 0)

    acc[...] = jnp.zeros_like(acc)
    yacc[...] = jnp.zeros_like(yacc)
    alive = [(s < cnt_ref[i]).astype(f32) for s in range(gk_ref.shape[1])]
    taps = [par(TAP0), par(TAP1), par(TAP2)]
    a2 = par(SLOPE_OUT)

    def chunk(k, _):
        r0 = pl.multiple_of(k * rows, rows)
        g_res = gr_ref[0, pl.ds(r0, rows), :]
        g_skip = alive[0] * gk_ref[0, 0, pl.ds(r0, rows), :]
        for s in range(1, len(alive)):
            g_skip = g_skip + alive[s] * gk_ref[0, s, pl.ds(r0, rows), :]
        m = mask_rows(start + r0, rows, length)
        both = jnp.concatenate([g_res, g_skip], axis=1)
        bias_ref[...] += fold(both)
        both = both * m
        acc[R_GM, :, 0 : 2 * base] += fold(both)
        ghi, glo = split(both)
        gs = dot(jnp.concatenate([ghi, ghi, glo], axis=1), wt3[...])
        his, los = [], []
        for j in range(width // LANES):
            s = slice(j * LANES, (j + 1) * LANES)
            f = (
                taps[0][:, s] * fst[pl.ds(r0, rows), s]
                + taps[1][:, s] * fst[pl.ds(r0 + TAP, rows), s]
                + taps[2][:, s] * fst[pl.ds(r0 + 2 * TAP, rows), s]
                + par(BIAS_DW)[:, s]
            )
            t = jnp.tanh(0.5 * f)
            a = a2[:, s]
            v = jnp.maximum(f, a * f) - ((1.0 - a) * LN2) * jnp.log2(0.5 + 0.5 * jnp.abs(t))
            dm = (0.5 + 0.5 * a) * m + ((0.5 - 0.5 * a) * m) * t

            @pl.when(k == 0)
            def _():
                acc[R_P, :, s] = jnp.broadcast_to(v[0:1], (8, LANES))

            d = v - acc[R_P, 0:1, s]
            g = gs[:, s]
            dd = d * m
            f0 = g * dm
            f2 = d * dm
            f0_ref[0, pl.ds(r0, rows), s] = f0
            f1_ref[0, pl.ds(r0, rows), s] = dm
            f2_ref[0, pl.ds(r0, rows), s] = f2
            acc[R_S, :, s] += fold(dd)
            acc[R_SS, :, s] += fold(dd * d)
            acc[R_GD, :, s] += fold(g * d)
            acc[R_GS, :, s] += fold(g)
            acc[R_H0, :, s] += fold(f0)
            acc[R_H1, :, s] += fold(dm)
            acc[R_H2, :, s] += fold(f2)
            acc[R_HF0, :, s] += fold(f0 * f)
            acc[R_HF1, :, s] += fold(dm * f)
            acc[R_HF2, :, s] += fold(f2 * f)
            acc[R_PF0, :, s] += fold(g * f)
            acc[R_PF1, :, s] += fold(m * f)
            acc[R_PF2, :, s] += fold(dd * f)
            hi, lo = split(d)
            his.append(hi)
            los.append(lo)
        hi, lo = jnp.concatenate(his, axis=1), jnp.concatenate(los, axis=1)
        z_ref[0, pl.ds(r0, rows), :] = dot(jnp.concatenate([hi, hi, lo], axis=1), wg3[...])
        yacc[...] += dot0(jnp.concatenate([ghi, ghi, glo], axis=0), jnp.concatenate([hi, lo, hi], axis=0))

        t0 = start + r0
        for row, near in ((R_A0, t0 < TAP), (R_Z0, (t0 < length) & (t0 + rows > length - TAP))):
            @pl.when(near)
            def _():
                at = lax.broadcasted_iota(jnp.int32, (rows, 1), 0) + t0
                edge = (at < TAP) if row == R_A0 else (at >= length - TAP)
                edge = edge.astype(f32)
                for q, ref in enumerate((f0_ref, f1_ref, f2_ref)):
                    acc[row + q] += fold(edge * ref[0, pl.ds(r0, rows), :])
        return 0

    lax.fori_loop(0, frames // rows, chunk, 0)
    y_ref[0] = yacc[...]
    sums = acc[...].sum(axis=1)
    point = acc[R_P, 0:1, :]
    ch_ref[0, 0:1, :] = point
    ch_ref[0, 1:ROWS, :] = sums[1:ROWS]

    def got(r):
        return sums[r : r + 1]

    n = jnp.clip(length - start, 0, frames).astype(f32)
    n_v = jnp.full((1, 1), n, f32)
    some = (n > 0).astype(f32)
    safe = jnp.maximum(n_v, 1.0)
    offset = got(R_S) / safe
    channel = point + offset
    mean2 = channel.sum(axis=1, keepdims=True) / width
    dev = channel - mean2
    spread = (got(R_SS) - safe * offset * offset + safe * dev * dev).sum(axis=1, keepdims=True)
    point = point - mean2
    gout = par(GAIN_OUT)
    wsum = taps[0] + taps[1] + taps[2]
    g1, sh1, cb = par(GAIN_IN), par(SHIFT_IN), par(BIAS_DW)

    def summed(x):
        return x.sum(axis=1, keepdims=True)

    s1 = summed(gout * got(R_GS))
    s2 = summed(gout * (got(R_GD) + point * got(R_GS)))
    t1, t2 = [], []
    for q in range(3):
        h, hf = got(R_H0 + q), got(R_HF0 + q)
        kh = wsum * h - taps[0] * got(R_A0 + q) - taps[2] * got(R_Z0 + q)
        if q == 0:
            h, hf, kh = gout * h, gout * hf, gout * kh
        if q == 2:
            h1, hf1 = got(R_H1), got(R_HF1)
            kh1 = wsum * h1 - taps[0] * got(R_A1) - taps[2] * got(R_Z1)
            h, hf, kh = h + point * h1, hf + point * hf1, kh + point * kh1
        t1.append(summed(g1 * kh))
        t2.append(summed(hf - cb * h - sh1 * kh))
    row = lane_put([mean2 * some, spread * some, n_v, s1, s2] + t1 + t2)
    st_ref[:, pl.ds(i, 1), :] = jnp.broadcast_to(row[None], (st_ref.shape[0], 1, LANES))


def third_kernel(
    rows, len_ref, tm_ref, v_ref, xb_ref, x_ref, xa_ref, f0_ref, f1_ref, f2_ref, gr_ref, z_ref, y_ref,
    ch_ref, bias_ref, w_ref, wr_ref, ws_ref, br_ref, pc_ref, ga1_ref, ga2_ref,
    res_ref, skip_ref, gin_ref, side_ref, sum_ref,
    w3, wt3, stat, coef, chan, zc, ext, vext, gw, gwt, acc,
):
    i = pl.program_id(0)
    items = pl.num_programs(0)
    frames, width = v_ref.shape[1:]
    base = gr_ref.shape[2]

    def par(k):
        return pc_ref[k : k + 1]

    def put(k, x):
        stat[k] = jnp.broadcast_to(x, stat.shape[1:])

    @pl.when(i == 0)
    def _():
        w3[...] = stacked3(w_ref[...])
        wt3[...] = stacked3(w_ref[...].T)
        mean1, scale1, count = merged(ga1_ref[...], width)
        mean2, scale2, _ = merged(ga2_ref[...], width)
        g = ga2_ref[...]

        def lane(k):
            return g[:, :, k : k + 1]

        dev = lane(0) - mean2[None]
        s1 = lane(3).sum(axis=0)
        s2 = (lane(4) + dev * lane(3)).sum(axis=0)
        alpha = scale2 * s1 / count
        beta = scale2 * scale2 * scale2 * s2 / count
        t1 = scale2 * lane(5).sum(axis=0) - alpha * lane(6).sum(axis=0) - beta * (lane(7) + dev * lane(6)).sum(axis=0)
        t2 = scale2 * lane(8).sum(axis=0) - alpha * lane(9).sum(axis=0) - beta * (lane(10) + dev * lane(9)).sum(axis=0)
        put(0, mean1)
        put(1, scale1)
        put(2, scale2)
        put(3, beta)
        put(4, scale1 * t1 / count)
        put(5, scale1 * scale1 * t2 / count)
        delta = ch_ref[:, R_P, :] - mean2
        coef[0] = scale2 * par(GAIN_OUT)
        coef[1] = alpha + beta * delta
        coef[2] = scale2 * par(GAIN_OUT) * delta + par(SHIFT_OUT)
        both = jnp.concatenate([wr_ref[...], ws_ref[...]], axis=1)
        zc[...] = lax.dot_general(
            coef[2], both, (((1,), (0,)), ((), ())), precision=lax.Precision.HIGHEST, preferred_element_type=f32
        )

        def row(r):
            return ch_ref[:, r, :]

        c0, c1 = coef[0], coef[1]

        def comb(r):
            return c0 * row(r) - c1 * row(r + 1) - beta * row(r + 2)

        h, hf, h_a, h_z = comb(R_H0), comb(R_HF0), comb(R_A0), comb(R_Z0)
        kh = (par(TAP0) + par(TAP1) + par(TAP2)) * h - par(TAP0) * h_a - par(TAP2) * h_z
        n = ga2_ref[pl.ds(tm_ref[0], 1), :, 2:3][0]
        total = c0 * row(R_GS) - c1 * n - beta * row(R_S)
        total_d = c0 * row(R_GD) - c1 * row(R_S) - beta * row(R_SS)
        total_f = c0 * row(R_PF0) - c1 * row(R_PF1) - beta * row(R_PF2)
        slope = (total_d + row(R_P) * total - total_f) / (1.0 - par(SLOPE_OUT))

        def over(x):
            return x.sum(axis=0, keepdims=True)

        gain_out = over(scale2 * row(R_GD) + (scale2 * delta) * row(R_GS))
        gain_in = over(hf - par(BIAS_DW) * h - par(SHIFT_IN) * kh) / par(GAIN_IN)
        shift = par(SHIFT_IN) - par(GAIN_IN) * scale1 * mean1
        chan[...] = jnp.concatenate(
            [jnp.zeros((2, width), f32), gain_in, over(kh), over(shift * (h - h_a)), over(shift * h),
             over(shift * (h - h_z)), over(h), -over(slope), gain_out, over(row(R_GS)), jnp.zeros((5, width), f32)],
            axis=0,
        )
        gw[...] = jnp.zeros_like(gw)
        gwt[...] = jnp.zeros_like(gwt)
        acc[...] = jnp.zeros_like(acc)

    length = len_ref[i]
    start = tm_ref[0] * frames

    def st(k):
        return wide(stat[k, pl.ds(i, 1), :], width)

    mean1, scale1, scale2, beta, cut, cut_v = [st(k) for k in range(6)]
    c0, c1 = coef[0, pl.ds(i, 1), :], coef[1, pl.ds(i, 1), :]
    gwt[...] += coef[0, pl.ds(i, 1), :] * y_ref[0]
    gain1 = par(GAIN_IN) * scale1
    taps = [par(TAP0), par(TAP1), par(TAP2)]
    a1 = par(SLOPE_IN)
    lead = TAP

    zeros = jnp.zeros((2 * TAP, width), f32)
    ext[0 : 2 * TAP, :] = zeros
    ext[frames + 2 * TAP : frames + 4 * TAP, :] = zeros

    def lift(k, _):
        r0 = pl.multiple_of(k * rows, rows)
        at = pl.ds(r0, rows)
        ext[pl.ds(2 * TAP + r0, rows), :] = c0 * f0_ref[0, at, :] - c1 * f1_ref[0, at, :] - beta * f2_ref[0, at, :]
        return 0

    lax.fori_loop(0, frames // rows, lift, 0)

    def part(x, at, rows, own, v_own):
        h = product3(x, w3[...]) + par(BIAS_IN)
        m = mask_rows(start + at - TAP, rows, length)
        xhi, xlo = split(x)
        his, los = [], []
        for j in range(width // LANES):
            s = slice(j * LANES, (j + 1) * LANES)
            hj, a = h[:, s], a1[:, s]
            t = jnp.tanh(0.5 * hj)
            logs = ((1.0 - a) * LN2) * jnp.log2(0.5 + 0.5 * jnp.abs(t))
            v = jnp.maximum(hj, a * hj) - logs
            later = ext[pl.ds(at + 2 * TAP, rows), s]
            here = ext[pl.ds(at + TAP, rows), s]
            before = ext[pl.ds(at, rows), s]
            vm = v * m
            acc[2, :, s] += gain1[:, s] * fold(later * vm)
            acc[3, :, s] += gain1[:, s] * fold(here * vm)
            acc[4, :, s] += gain1[:, s] * fold(before * vm)
            u = taps[0][:, s] * later + taps[1][:, s] * here + taps[2][:, s] * before
            u = gain1[:, s] * u
            if own:
                u = u - cut[:, s] - cut_v[:, s] * (v - mean1[:, s])
            u = u * m
            acc[1, :, s] += fold(u * (v - hj))
            gh = u * ((0.5 + 0.5 * a) + (0.5 - 0.5 * a) * t)
            acc[0, :, s] += fold(gh)
            hi, lo = split(gh)
            his.append(hi)
            los.append(lo)
        hi, lo = jnp.concatenate(his, axis=1), jnp.concatenate(los, axis=1)
        gw[...] += dot0(jnp.concatenate([xhi, xhi, xlo], axis=0), jnp.concatenate([hi, lo, hi], axis=0))
        return dot(jnp.concatenate([hi, hi, lo], axis=1), wt3[...])

    side_ref[0, 0] = part(xb_ref[0], 0, TAP, False, None)
    side_ref[1, 0] = part(xa_ref[0], frames + TAP, TAP, False, None)

    scale_c = stat[2, pl.ds(i, 1), :]

    def chunk(k, _):
        r0 = pl.multiple_of(k * rows, rows)
        at = pl.ds(r0, rows)
        x = x_ref[0, at, :]
        back = part(x, r0 + TAP, rows, True, None)
        gin_ref[0, at, :] = gr_ref[0, at, :] + back
        m = mask_rows(start + r0, rows, length)
        z = z_ref[0, at, :]
        zi = zc[pl.ds(i, 1), :]
        res_ref[0, at, :] = x + m * (scale_c * z[:, 0:base] + zi[:, 0:base]) + br_ref[0:1, :]
        skip_ref[0, at, :] = m * (scale_c * z[:, base:] + zi[:, base:]) + br_ref[1:2, :]
        return 0

    lax.fori_loop(0, frames // rows, chunk, 0)

    @pl.when(i == items - 1)
    def _():
        outer = lax.dot_general(
            ch_ref[:, R_GM, 0 : 2 * base], coef[2], (((0,), (0,)), ((), ())),
            precision=lax.Precision.HIGHEST, preferred_element_type=f32,
        )
        both = (gwt[...] + outer).T
        sum_ref[0:width, :] = both[:, 0:base]
        sum_ref[width : 2 * width, :] = both[:, base:]
        for j in range(width // LANES):
            sum_ref[2 * width + j * base : 2 * width + (j + 1) * base, :] = gw[:, j * LANES : (j + 1) * LANES]
        done = acc[...].sum(axis=1)
        rows_ = chan[...]
        extra = jnp.concatenate(
            [done[0:1], -done[1:2] / (1.0 - par(SLOPE_IN)), jnp.zeros((2, width), f32), done[2:5],
             jnp.zeros((9, width), f32)], axis=0)
        rows_ = rows_ + extra
        at0 = 2 * width + 4 * base
        for j in range(width // LANES):
            sum_ref[at0 + j * 16 : at0 + (j + 1) * 16, :] = rows_[:, j * LANES : (j + 1) * LANES]
        at1 = at0 + 64
        bias = bias_ref[...].sum(axis=0, keepdims=True)
        tail = jnp.concatenate([bias[:, 0:base], bias[:, base:], jnp.zeros((6, base), f32)], axis=0)
        sum_ref[at1 : at1 + 8, :] = tail
        sum_ref[at1 + 8 :, :] = jnp.zeros((sum_ref.shape[0] - at1 - 8, LANES), f32)


def sum_rows(size):
    return -(-size // 256) * 256


def exchange(x, axis):
    return lax.all_to_all(x, axis, 0, 0)


def reduce_all(x, sizes):
    steps = []
    for axis in ("item", "tm"):
        by = 1
        while by < sizes[axis]:
            steps.append((axis, by))
            by *= 2
    order = sorted(steps, key=lambda s: (s[1], s[0]))

    def swap(y, axis, by):
        return lax.ppermute(y, axis, [(d, d ^ by) for d in range(sizes[axis])])

    for axis, by in order:
        half = x.shape[0] // 2
        mine = (lax.axis_index(axis) // by) % 2
        keep = lax.dynamic_slice_in_dim(x, mine * half, half)
        send = lax.dynamic_slice_in_dim(x, (1 - mine) * half, half)
        x = keep + swap(send, axis, by)
    for axis, by in order[::-1]:
        mine = (lax.axis_index(axis) // by) % 2
        other = swap(x, axis, by)
        x = jnp.where(mine == 0, jnp.concatenate([x, other]), jnp.concatenate([other, x]))
    return x


def whole(shape):
    return pl.BlockSpec(shape, lambda i: (0,) * len(shape))


def per_item(shape):
    return pl.BlockSpec((1,) + shape, lambda i: (i,) + (0,) * len(shape))


SMEM = pl.BlockSpec(memory_space=pltpu.SMEM)


def body(
    inputs, lengths, counts, weight_in, bias_in, slope_in, gain_in, shift_in, channelwise_taps, channelwise_bias,
    slope_out, gain_out, shift_out, weight_res, bias_res, weight_skip, bias_skip, grad_residual, grad_skip,
):
    items, frames, base = inputs.shape
    width = weight_in.shape[1]
    sources = grad_skip.shape[1]
    tm, across = lax.axis_size("tm"), lax.axis_size("item")
    place = lax.axis_index("tm").astype(jnp.int32).reshape(1)
    up = [(d, d + 1) for d in range(tm - 1)]
    down = [(d + 1, d) for d in range(tm - 1)]
    x_before = lax.ppermute(inputs[:, frames - TAP :], "tm", up)
    x_after = lax.ppermute(inputs[:, :TAP], "tm", down)

    table = jnp.concatenate(
        [jnp.stack([bias_in, slope_in, gain_in, shift_in]), channelwise_taps,
         jnp.stack([channelwise_bias, slope_out, gain_out, shift_out]), jnp.zeros((5, width), f32)], axis=0)
    params = pltpu.CompilerParams(vmem_limit_bytes=VMEM)

    v1, st1 = pl.pallas_call(
        functools.partial(first_kernel, min(512, frames)),
        grid=(items,),
        in_specs=[SMEM, SMEM, per_item((frames, base)), whole((base, width)), whole((16, width))],
        out_specs=[per_item((frames, width)), whole((tm, items, LANES))],
        out_shape=[jax.ShapeDtypeStruct((items, frames, width), f32), jax.ShapeDtypeStruct((tm, items, LANES), f32)],
        scratch_shapes=[pltpu.VMEM((3 * base, width), bf16)],
        compiler_params=params,
        name="first",
    )(lengths, place, inputs, weight_in, table)
    ga1 = exchange(st1, "tm")

    rows = 256
    big = jax.ShapeDtypeStruct((items, frames, width), f32)
    f0, f1, f2, z, y, ch, st2, bias = pl.pallas_call(
        functools.partial(second_kernel, rows),
        grid=(items,),
        in_specs=[SMEM, SMEM, SMEM, per_item((frames, width)), per_item((TAP, base)), per_item((TAP, base)),
                  per_item((frames, base)), per_item((sources, frames, base)), whole((base, width)),
                  whole((width, base)), whole((width, base)), whole((16, width)), whole((tm, items, LANES))],
        out_specs=[per_item((frames, width))] * 3 + [per_item((frames, 2 * base)), per_item((2 * base, width)),
                   per_item((ROWS, width)), whole((tm, items, LANES)), whole((8, 2 * base))],
        out_shape=[big, big, big, jax.ShapeDtypeStruct((items, frames, 2 * base), f32),
                   jax.ShapeDtypeStruct((items, 2 * base, width), f32), jax.ShapeDtypeStruct((items, ROWS, width), f32),
                   jax.ShapeDtypeStruct((tm, items, LANES), f32), jax.ShapeDtypeStruct((8, 2 * base), f32)],
        scratch_shapes=[pltpu.VMEM((3 * base, width), bf16), pltpu.VMEM((6 * base, width), bf16),
                        pltpu.VMEM((3 * width, 2 * base), bf16), pltpu.VMEM((2, items, LANES), f32),
                        pltpu.VMEM((frames + 2 * TAP, width), f32), pltpu.VMEM((8, LANES), f32),
                        pltpu.VMEM((8, LANES), f32), pltpu.VMEM((ROWS, 8, width), f32),
                        pltpu.VMEM((2 * base, width), f32)],
        compiler_params=params,
        name="second",
    )(lengths, counts, place, v1, x_before, x_after, grad_residual, grad_skip, weight_in, weight_res, weight_skip,
      table, ga1)
    ga2 = exchange(st2, "tm")

    n_sum = sum_rows(2 * width + 4 * base + 64 + 8)
    out = jax.ShapeDtypeStruct((items, frames, base), f32)
    biases = jnp.stack([bias_res, bias_skip])
    res, skip, gin, side, sums = pl.pallas_call(
        functools.partial(third_kernel, rows),
        grid=(items,),
        in_specs=[SMEM, SMEM, per_item((frames, width)), per_item((TAP, base)), per_item((frames, base)),
                  per_item((TAP, base)), per_item((frames, width)), per_item((frames, width)),
                  per_item((frames, width)), per_item((frames, base)), per_item((frames, 2 * base)),
                  per_item((2 * base, width)), whole((items, ROWS, width)), whole((8, 2 * base)),
                  whole((base, width)), whole((width, base)), whole((width, base)), whole((2, base)),
                  whole((16, width)), whole((tm, items, LANES)), whole((tm, items, LANES))],
        out_specs=[per_item((frames, base))] * 3 + [pl.BlockSpec((2, 1, TAP, base), lambda i: (0, i, 0, 0)),
                   whole((n_sum, base))],
        out_shape=[out, out, out, jax.ShapeDtypeStruct((2, items, TAP, base), f32),
                   jax.ShapeDtypeStruct((n_sum, base), f32)],
        scratch_shapes=[pltpu.VMEM((3 * base, width), bf16), pltpu.VMEM((3 * width, base), bf16),
                        pltpu.VMEM((6, items, LANES), f32), pltpu.VMEM((3, items, width), f32),
                        pltpu.VMEM((16, width), f32), pltpu.VMEM((items, 2 * base), f32),
                        pltpu.VMEM((frames + 4 * TAP, width), f32), pltpu.VMEM((8, LANES), f32),
                        pltpu.VMEM((base, width), f32), pltpu.VMEM((2 * base, width), f32),
                        pltpu.VMEM((8, 8, width), f32)],
        compiler_params=params,
        name="third",
    )(lengths, place, v1, x_before, inputs, x_after, f0, f1, f2, grad_residual, z, y, ch, bias, weight_in, weight_res,
      weight_skip, biases, table, ga1, ga2)

    from_next = lax.ppermute(side[0], "tm", down)
    from_last = lax.ppermute(side[1], "tm", up)
    total = reduce_all(sums, {"tm": tm, "item": across})
    gin = gin.at[:, frames - TAP :].add(from_next)
    gin = gin.at[:, :TAP].add(from_last)

    g_res, g_skip = total[0:width], total[width : 2 * width]
    at0 = 2 * width + 4 * base
    g_in = total[2 * width : at0].reshape(4, base, LANES).transpose(1, 0, 2).reshape(base, width)
    vec = total[at0 : at0 + 64].reshape(4, 16, LANES).transpose(1, 0, 2).reshape(16, width)
    return (
        res, skip, gin, g_in, vec[0], vec[1], vec[2], vec[3], vec[4:7], vec[7], vec[8], vec[9], vec[10],
        g_res, total[at0 + 64], g_skip, total[at0 + 65],
    )


def solution(mesh):
    spread = P("item", "tm", None)
    return jax.shard_map(
        body,
        mesh=mesh,
        in_specs=(spread, P("item"), P("item")) + (P(),) * 14 + (spread, P("item", None, "tm", None)),
        out_specs=(spread,) * 3 + (P(),) * 14,
        check_vma=False,
    )
```

```python
import functools

import jax
import jax.numpy as jnp
from jax import lax
from jax.experimental import pallas as pl
from jax.experimental.pallas import tpu as pltpu
from jax.sharding import PartitionSpec as P

TAP = 128
LANES = 128
EPSILON = 1e-05
LN2 = 0.6931471805599453
f32 = jnp.float32
bf16 = jnp.bfloat16

PARAMS = ("bias_in", "slope_in", "gain_in", "shift_in", "taps", "bias_dw", "slope_out", "gain_out", "shift_out")
(R_P, R_S, R_SS, R_GD, R_GS, R_H0, R_H1, R_H2, R_HF0, R_HF1, R_HF2, R_PF0, R_PF1, R_PF2,
 R_A0, R_A1, R_A2, R_Z0, R_Z1, R_Z2, R_GM) = range(21)
ROWS = 24
SUB = 32
HALF = 128
CHUNK1, CHUNK2, CHUNK3 = 256, 256, 256


def split(x):
    hi = x.astype(bf16)
    lo = (x - hi.astype(f32)).astype(bf16)
    return hi, lo


def dot(a, b):
    return jnp.dot(a, b, preferred_element_type=f32)


def dot0(a, b):
    return lax.dot_general(a, b, (((0,), (0,)), ((), ())), preferred_element_type=f32)


def product3(x, w3):
    hi, lo = split(x)
    return dot(jnp.concatenate([hi, hi, lo], axis=1), w3)


def stacked3(w):
    hi, lo = split(w)
    return jnp.concatenate([hi, lo, hi], axis=0)


def half_act(h, a, c):
    t = jnp.tanh(h)
    return jnp.maximum(h, a * h) - c * jnp.log2(1.0 + jnp.abs(t)), t


def fold(x):
    rows, cols = x.shape
    return x.reshape(rows // 8, 8, cols).sum(axis=0)


def mask_rows(first, rows, length):
    row = lax.broadcasted_iota(jnp.int32, (rows, 1), 0) + first
    return ((row >= 0) & (row < length)).astype(f32)


def lane_put(values):
    shape = values[0].shape[:-1] + (LANES,)
    lane = lax.broadcasted_iota(jnp.int32, shape, len(shape) - 1)
    out = jnp.zeros(shape, f32)
    for k, v in enumerate(values):
        out = jnp.where(lane == k, jnp.broadcast_to(v, shape), out)
    return out


def channel(ref):
    def get(name):
        if name.startswith("tap"):
            k = int(name[3])
            return ref["taps"][k : k + 1]
        return ref[name][...]

    return get


def interleave(first, second):
    done = 0
    for n, piece in enumerate(first):
        piece()
        upto = (n + 1) * len(second) // len(first)
        for other in second[done:upto]:
            other()
        done = upto
    for other in second[done:]:
        other()


def blocks(width):
    return [slice(j * LANES, (j + 1) * LANES) for j in range(width // LANES)]


def per_item_column(values):
    row = lax.broadcasted_iota(jnp.int32, (len(values), 1), 0)
    out = jnp.zeros((len(values), 1), f32)
    for k, v in enumerate(values):
        out = jnp.where(row == k, v, out)
    return out


def frames_here(len_ref, start, frames, items):
    return per_item_column([jnp.clip(len_ref[k] - start, 0, frames).astype(f32) for k in range(items)])


def first_kernel(rows, len_ref, tm_ref, x_ref, xn_ref, w_ref, b_ref, a_ref, v_ref, st_ref, ch_ref, w3, acc, hb0, hb1):
    i = pl.program_id(0)
    items = ch_ref.shape[0]
    frames, width = v_ref.shape[1:]
    slots = (hb0, hb1)

    @pl.when(i == 0)
    def _():
        w3[...] = stacked3(0.5 * w_ref[...])
        hb0[...] = product3(x_ref[0, 0:rows, :], w3[...])

    length = len_ref[i]
    start = tm_ref[0] * frames
    b, a = 0.5 * b_ref[...], a_ref[...]
    c = (1.0 - a) * (0.5 * LN2)
    centre = half_act(hb0[0:8, :] + b, a, c)[0][0:1]
    parts = frames // rows

    for k in range(parts):
        def step(masked, k=k):
            h, then = slots[k % 2], slots[(k + 1) % 2]
            if masked:
                m = mask_rows(start + k * rows, rows, length)

            def ahead(q):
                x = x_ref[0, (k + 1) * rows + q : (k + 1) * rows + q + HALF, :] if k < parts - 1 else xn_ref[0, q : q + HALF, :]
                then[q : q + HALF, :] = product3(x, w3[...])

            def unit(s):
                total = square = jnp.zeros((8, LANES), f32)
                for q in range(0, rows, SUB):
                    v, _ = half_act(h[q : q + SUB, s] + b[:, s], a[:, s], c[:, s])
                    v_ref[0, k * rows + q : k * rows + q + SUB, s] = v
                    d = v - centre[:, s]
                    dm = d * m[q : q + SUB] if masked else d
                    total = total + fold(dm)
                    square = square + fold(dm * d)
                acc[0, :, s] = total if k == 0 else acc[0, :, s] + total
                acc[1, :, s] = square if k == 0 else acc[1, :, s] + square

            interleave([functools.partial(ahead, q) for q in range(0, rows, HALF)],
                       [functools.partial(unit, s) for s in blocks(width)])

        full = start + (k + 1) * rows <= length
        pl.when(full)(functools.partial(step, False))
        pl.when(jnp.logical_not(full))(functools.partial(step, True))

    ch_ref[pl.ds(i, 1), 0, :] = acc[0].sum(axis=0, keepdims=True)
    ch_ref[pl.ds(i, 1), 1, :] = acc[1].sum(axis=0, keepdims=True)
    ch_ref[pl.ds(i, 1), 2, :] = centre

    @pl.when(i == items - 1)
    def _():
        n = frames_here(len_ref, start, frames, items)
        safe = jnp.maximum(n, 1.0)
        total, square, centre = ch_ref[:, 0, :], ch_ref[:, 1, :], ch_ref[:, 2, :]
        ch_ref[:, 0, :] = total + n * centre
        ch_ref[:, 1, :] = square + 2.0 * centre * total + n * centre * centre
        total = total / safe
        level = centre + c + total
        mean = level.sum(axis=1, keepdims=True) / width
        dev = level - mean
        spread = (square - safe * total * total + safe * dev * dev).sum(axis=1, keepdims=True)
        some = (n > 0).astype(f32)
        st_ref[...] = jnp.broadcast_to(lane_put([2.0 * mean * some, 4.0 * spread * some, n])[None], st_ref.shape)


def merged(gathered, width):
    mean_d, spread_d, n_d = gathered[:, :, 0:1], gathered[:, :, 1:2], gathered[:, :, 2:3]
    n = n_d.sum(axis=0)
    mean = (n_d * mean_d).sum(axis=0) / n
    dev = mean_d - mean[None]
    spread = (spread_d + n_d * width * dev * dev).sum(axis=0)
    count = n * width
    return mean, lax.rsqrt(spread / count + EPSILON), count


def wide(x, width):
    return jnp.broadcast_to(x[:, 0:1], (x.shape[0], width))


def second_kernel(
    rows, len_ref, cnt_ref, tm_ref, v_ref, xb_ref, xa_ref, gr_ref, gk_ref, w_ref, wr_ref, ws_ref, *rest
):
    params, rest = rest[: len(PARAMS)], rest[len(PARAMS) :]
    ga_ref, f0_ref, f1_ref, f2_ref, z_ref, y_ref, ch_ref, st_ref, bias_ref, *rest = rest
    w3, wt3, wg3, stat, fst, acc, gacc, yacc, gs0, gs1, hl0, hl1, gb = rest
    par = channel(dict(zip(PARAMS, params)))
    i = pl.program_id(0)
    items = ch_ref.shape[0]
    frames, width = v_ref.shape[1:]
    base = gr_ref.shape[2]
    parts = frames // rows
    gs_slots, hl_slots = (gs0, gs1), (hl0, hl1)

    @pl.when(i == 0)
    def _():
        w3[...] = stacked3(0.5 * w_ref[...])
        both = jnp.concatenate([wr_ref[...], ws_ref[...]], axis=1)
        wt3[...] = stacked3(both.T)
        gain = 2.0 * par("gain_out")
        wg3[...] = stacked3((both.T * gain).T)
        mean, scale, _ = merged(ga_ref[...], width)
        stat[0] = jnp.broadcast_to(mean, stat.shape[1:])
        stat[1] = jnp.broadcast_to(scale, stat.shape[1:])
        bias_ref[...] = jnp.zeros_like(bias_ref)
        ch_ref[...] = jnp.zeros_like(ch_ref)

    length = len_ref[i]
    start = tm_ref[0] * frames
    mean = wide(stat[0, pl.ds(i, 1), :], width)
    scale = wide(stat[1, pl.ds(i, 1), :], width)
    a1 = par("slope_in")
    c1 = (1.0 - a1) * (0.5 * LN2)
    gain = 2.0 * par("gain_in") * scale
    shift = par("shift_in") + gain * (c1 - 0.5 * mean)
    b1 = 0.5 * par("bias_in")
    alive = [(s < cnt_ref[i]).astype(f32) for s in range(gk_ref.shape[1])]
    taps = [0.5 * par(f"tap{k}") for k in range(3)]
    bias = 0.5 * par("bias_dw")
    a2 = par("slope_out")
    c2 = (1.0 - a2) * (0.5 * LN2)
    d_base, d_gain = 0.5 + 0.5 * a2, 0.5 - 0.5 * a2

    def cotangents(k):
        at = slice(k * rows, (k + 1) * rows)
        g_res = gr_ref[0, at, :]
        g_skip = alive[0] * gk_ref[0, 0, at, :]
        for s in range(1, len(alive)):
            g_skip = g_skip + alive[s] * gk_ref[0, s, at, :]
        return jnp.concatenate([g_res, g_skip], axis=1)

    def spread(k):
        def prepare():
            both = cotangents(k)
            bias_ref[...] += fold(both)
            row = lax.broadcasted_iota(jnp.int32, (rows, 1), 0)
            both = jnp.where(row < length - start - k * rows, both, 0.0)
            gacc[...] = fold(both) if k == 0 else gacc[...] + fold(both)
            ghi, glo = split(both)
            gb[k, 0], gb[k, 1] = ghi, glo

        def multiply(q):
            if q == 0:
                prepare()
            ghi, glo = gb[k, 0, q : q + HALF, :], gb[k, 1, q : q + HALF, :]
            gs_slots[k % 2][q : q + HALF, :] = dot(jnp.concatenate([ghi, ghi, glo], axis=1), wt3[...])

        return [functools.partial(multiply, q) for q in range(0, rows, HALF)]

    def products(k):
        hl = hl_slots[k % 2]

        def out(q):
            hi, lo = hl[0, q : q + HALF, :], hl[1, q : q + HALF, :]
            z_ref[0, k * rows + q : k * rows + q + HALF, :] = dot(jnp.concatenate([hi, hi, lo], axis=1), wg3[...])

        def weights(q):
            at = slice(q, q + base)
            ghi, glo = gb[k, 0, :, at], gb[k, 1, :, at]
            y = dot0(jnp.concatenate([ghi, ghi, glo], axis=0), jnp.concatenate([hl[0], hl[1], hl[0]], axis=0))
            if k == parts - 1:
                y_ref[0, at, :] = yacc[at, :] + y if k else y
            else:
                yacc[at, :] = yacc[at, :] + y if k else y

        return [functools.partial(out, q) for q in range(0, rows, HALF)] + [
            functools.partial(weights, q) for q in (0, base)]

    h = product3(jnp.concatenate([xb_ref[0], xa_ref[0]], axis=0), w3[...])
    for piece in spread(0):
        piece()
    for side, at in ((0, 0), (1, frames + TAP)):
        m = mask_rows(start + at - TAP, TAP, length)
        for s in blocks(width):
            for q in range(0, TAP, SUB):
                v, _ = half_act(h[side * TAP + q : side * TAP + q + SUB, s] + b1[:, s], a1[:, s], c1[:, s])
                fst[at + q : at + q + SUB, s] = m[q : q + SUB] * (gain[:, s] * v + shift[:, s])

    def lift(k, _):
        r0 = pl.multiple_of(k * TAP, TAP)
        full = start + r0 + TAP <= length

        @pl.when(full)
        def _():
            fst[pl.ds(TAP + r0, TAP), :] = gain * v_ref[0, pl.ds(r0, TAP), :] + shift

        @pl.when(jnp.logical_not(full))
        def _():
            m = mask_rows(start + r0, TAP, length)
            fst[pl.ds(TAP + r0, TAP), :] = m * (gain * v_ref[0, pl.ds(r0, TAP), :] + shift)

        return 0

    lax.fori_loop(0, frames // TAP, lift, 0)

    def halved(r, size, s):
        return (
            taps[0][:, s] * fst[r : r + size, s]
            + taps[1][:, s] * fst[r + TAP : r + TAP + size, s]
            + taps[2][:, s] * fst[r + 2 * TAP : r + 2 * TAP + size, s]
            + bias[:, s]
        )

    point = jnp.concatenate(
        [half_act(halved(0, 8, s), a2[:, s], c2[:, s])[0][0:1] for s in blocks(width)], axis=1
    )
    tracked = [r for r in range(R_S, R_A0) if r != R_GS]

    def elementwise(k, masked):
        gs, hl = gs_slots[k % 2], hl_slots[k % 2]
        if masked:
            m = mask_rows(start + k * rows, rows, length)

        def unit(s, begin):
            zero = jnp.zeros((8, LANES), f32)
            sums = {r: zero for r in tracked}
            for q in range(begin, begin + HALF, SUB):
                at = slice(k * rows + q, k * rows + q + SUB)
                f = halved(k * rows + q, SUB, s)
                v, t = half_act(f, a2[:, s], c2[:, s])
                dm = d_base[:, s] + d_gain[:, s] * t
                d = v - point[:, s]
                g = gs[q : q + SUB, s]
                dd, fm = d, f
                if masked:
                    mq = m[q : q + SUB]
                    dm, dd, fm = dm * mq, d * mq, f * mq
                f0 = g * dm
                f2 = d * dm
                f0_ref[0, at, s] = f0
                f1_ref[0, at, s] = dm
                f2_ref[0, at, s] = f2
                for r, x in (
                    (R_S, dd), (R_SS, dd * d), (R_GD, g * d), (R_H0, f0), (R_H1, dm), (R_H2, f2), (R_HF0, f0 * f),
                    (R_HF1, dm * f), (R_HF2, f2 * f), (R_PF0, g * f), (R_PF1, fm), (R_PF2, dd * f),
                ):
                    sums[r] = sums[r] + fold(x)
                hi, lo = split(d)
                hl[0, q : q + SUB, s] = hi
                hl[1, q : q + SUB, s] = lo
            for r, x in sums.items():
                acc[r, :, s] = x if k == 0 and begin == 0 else acc[r, :, s] + x

        return [functools.partial(unit, s, q) for q in range(0, rows, HALF) for s in blocks(width)]

    def nothing(k):
        at = slice(k * rows, (k + 1) * rows)
        zero = jnp.zeros((rows, width), f32)
        for ref in (f0_ref, f1_ref, f2_ref):
            ref[0, at, :] = zero
        hl_slots[k % 2][...] = jnp.zeros_like(hl0)
        if k == 0:
            for r in tracked:
                acc[r] = jnp.zeros((8, width), f32)

    for k in range(parts):
        def step(kind, k=k):
            matrix = (spread(k + 1) if k + 1 < parts else []) + (products(k - 1) if k > 0 else [])
            interleave(matrix, [functools.partial(nothing, k)] if kind == "none" else elementwise(k, kind == "some"))

        t0 = start + k * rows
        full, none = t0 + rows <= length, t0 >= length
        pl.when(full)(functools.partial(step, "full"))
        pl.when(jnp.logical_not(full | none))(functools.partial(step, "some"))
        pl.when(none)(functools.partial(step, "none"))
    for piece in products(parts - 1):
        piece()

    edges = acc.at[pl.ds(R_A0, 6)]
    edges[...] = jnp.zeros(edges.shape, f32)

    def edge(k, _):
        r0 = pl.multiple_of(k * TAP, TAP)
        t0 = start + r0
        for row, near in ((R_A0, t0 < TAP), (R_Z0, (t0 < length) & (t0 + TAP > length - TAP))):
            @pl.when(near)
            def _():
                at = lax.broadcasted_iota(jnp.int32, (TAP, 1), 0) + t0
                there = ((at < TAP) if row == R_A0 else (at >= length - TAP)).astype(f32)
                for q, ref in enumerate((f0_ref, f1_ref, f2_ref)):
                    acc[row + q] += fold(there * ref[0, pl.ds(r0, TAP), :])
        return 0

    lax.fori_loop(0, frames // TAP, edge, 0)

    ch_ref[pl.ds(i, 1), R_GM, 0 : 2 * base] = gacc[...].sum(axis=0, keepdims=True)
    ch_ref[pl.ds(i, 1), R_P, :] = 2.0 * (point + c2)
    for r in range(R_S, R_GM):
        if r != R_GS:
            total = acc[r].sum(axis=0, keepdims=True)
            if r in (R_S, R_GD, R_H2, R_HF0, R_HF1, R_PF0, R_PF1, R_A2, R_Z2):
                total = 2.0 * total
            if r in (R_SS, R_HF2, R_PF2):
                total = 4.0 * total
            ch_ref[pl.ds(i, 1), r, :] = total

    @pl.when(i == items - 1)
    def _():
        gm = jnp.concatenate([ch_ref[:, R_GM, 0 : 2 * base]] * 2, axis=0)
        ch_ref[:, R_GS, :] = product3(gm, wt3[...])[0:items]

        def got(r):
            return ch_ref[:, r, :]

        n = frames_here(len_ref, start, frames, items)
        some = (n > 0).astype(f32)
        safe = jnp.maximum(n, 1.0)
        point, offset = got(R_P), got(R_S) / safe
        level = point + offset
        mean2 = level.sum(axis=1, keepdims=True) / width
        dev = level - mean2
        spread2 = (got(R_SS) - safe * offset * offset + safe * dev * dev).sum(axis=1, keepdims=True)
        point = point - mean2
        gout = par("gain_out")
        tap0, tap1, tap2 = par("tap0"), par("tap1"), par("tap2")
        g1, sh1, cb = par("gain_in"), par("shift_in"), par("bias_dw")

        def summed(x):
            return x.sum(axis=1, keepdims=True)

        s1 = summed(gout * got(R_GS))
        s2 = summed(gout * (got(R_GD) + point * got(R_GS)))
        t1, t2 = [], []
        for q in range(3):
            h, hf, h_a, h_z = got(R_H0 + q), got(R_HF0 + q), got(R_A0 + q), got(R_Z0 + q)
            if q == 0:
                h, hf, h_a, h_z = gout * h, gout * hf, gout * h_a, gout * h_z
            if q == 2:
                h, hf = h + point * got(R_H1), hf + point * got(R_HF1)
                h_a, h_z = h_a + point * got(R_A1), h_z + point * got(R_Z1)
            kh = (tap0 + tap1 + tap2) * h - tap0 * h_a - tap2 * h_z
            t1.append(summed(g1 * kh))
            t2.append(summed(hf - cb * h - sh1 * kh))
        row = lane_put([mean2 * some, spread2 * some, n, s1, s2] + t1 + t2)
        st_ref[...] = jnp.broadcast_to(row[None], st_ref.shape)


def edge_kernel(
    frames, len_ref, tm_ref, xb_ref, xa_ref, f0a_ref, f0z_ref, f1a_ref, f1z_ref, f2a_ref, f2z_ref,
    ch1_ref, ch_ref, w_ref, wr_ref, ws_ref, *rest
):
    params, rest = rest[: len(PARAMS)], rest[len(PARAMS) :]
    ga1_ref, ga2_ref, before_ref, after_ref, stat_ref, coef_ref, chan_ref, zc_ref, gw, acc, w3, wt3 = rest
    par = channel(dict(zip(PARAMS, params)))
    i = pl.program_id(0)
    width = f0a_ref.shape[2]
    tap0, tap1, tap2 = par("tap0"), par("tap1"), par("tap2")
    a1 = par("slope_in")
    c1 = (1.0 - a1) * (0.5 * LN2)

    def put(k, x):
        stat_ref[k] = jnp.broadcast_to(x, stat_ref.shape[1:])

    @pl.when(i == 0)
    def _():
        w3[...] = stacked3(0.5 * w_ref[...])
        wt3[...] = stacked3(w_ref[...].T)
        mean1, scale1, count = merged(ga1_ref[...], width)
        mean2, scale2, _ = merged(ga2_ref[...], width)
        g = ga2_ref[...]

        def lane(k):
            return g[:, :, k : k + 1]

        dev = lane(0) - mean2[None]
        s1 = lane(3).sum(axis=0)
        s2 = (lane(4) + dev * lane(3)).sum(axis=0)
        alpha = scale2 * s1 / count
        beta = scale2 * scale2 * scale2 * s2 / count
        t1 = scale2 * lane(5).sum(axis=0) - alpha * lane(6).sum(axis=0) - beta * (lane(7) + dev * lane(6)).sum(axis=0)
        t2 = scale2 * lane(8).sum(axis=0) - alpha * lane(9).sum(axis=0) - beta * (lane(10) + dev * lane(9)).sum(axis=0)
        cut = scale1 * t1 / count
        cut_v = scale1 * scale1 * t2 / count
        put(0, scale1)
        put(1, scale2)
        put(2, 2.0 * beta)
        put(3, cut - cut_v * mean1)
        put(4, 2.0 * cut_v)
        delta = ch_ref[:, R_P, :] - mean2
        coef_ref[0] = scale2 * par("gain_out")
        coef_ref[1] = alpha + beta * delta
        coef_ref[2] = scale2 * par("gain_out") * delta + par("shift_out")
        both = jnp.concatenate([wr_ref[...], ws_ref[...]], axis=1)
        zc_ref[...] = lax.dot_general(
            coef_ref[2], both, (((1,), (0,)), ((), ())), precision=lax.Precision.HIGHEST, preferred_element_type=f32
        )

        def row(r):
            return ch_ref[:, r, :]

        c0, cc = coef_ref[0], coef_ref[1]

        def comb(r):
            return c0 * row(r) - cc * row(r + 1) - beta * row(r + 2)

        h, hf, h_a, h_z = comb(R_H0), comb(R_HF0), comb(R_A0), comb(R_Z0)
        kh = (tap0 + tap1 + tap2) * h - tap0 * h_a - tap2 * h_z
        n = ga2_ref[pl.ds(tm_ref[0], 1), :, 2:3][0]
        total = c0 * row(R_GS) - cc * n - beta * row(R_S)
        total_d = c0 * row(R_GD) - cc * row(R_S) - beta * row(R_SS)
        total_f = c0 * row(R_PF0) - cc * row(R_PF1) - beta * row(R_PF2)
        slope = (total_d + row(R_P) * total - total_f) / (1.0 - par("slope_out"))

        def over(x):
            return x.sum(axis=0, keepdims=True)

        gain_out = over(scale2 * row(R_GD) + (scale2 * delta) * row(R_GS))
        gain_in = over(hf - par("bias_dw") * h - par("shift_in") * kh) / par("gain_in")
        gain1 = par("gain_in") * scale1
        shift = par("shift_in") + gain1 * (2.0 * c1 - mean1)
        m1, m2 = ch1_ref[:, 0, :], ch1_ref[:, 1, :]
        k0 = cut - cut_v * mean1 + 2.0 * cut_v * c1
        k1 = 2.0 * cut_v
        act_sum = gain1 * kh - k0 * n - k1 * m1
        act_v = -(k0 * m1 + k1 * m2)
        zero = jnp.zeros((1, width), f32)
        chan_ref[...] = jnp.concatenate(
            [zero, over(c1 * act_sum + act_v), gain_in, over(kh), over(shift * (h - h_a)), over(shift * h),
             over(shift * (h - h_z)), over(h), -over(slope), gain_out, over(row(R_GS)), jnp.zeros((5, width), f32)],
            axis=0,
        )
        gw[...] = jnp.zeros_like(gw)
        acc[...] = jnp.zeros_like(acc)

    length = len_ref[i]
    start = tm_ref[0] * frames

    def st(k):
        return wide(stat_ref[k, pl.ds(i, 1), :], width)

    gain1, beta = par("gain_in") * st(0), st(2)
    c0, cc = coef_ref[0, pl.ds(i, 1), :], coef_ref[1, pl.ds(i, 1), :]
    b1 = 0.5 * par("bias_in")
    d_base, d_gain = 0.5 + 0.5 * a1, 0.5 - 0.5 * a1
    x = jnp.concatenate([xb_ref[0], xa_ref[0]], axis=0)
    xhi, xlo = split(x)
    h = dot(jnp.concatenate([xhi, xhi, xlo], axis=1), w3[...])
    masks = (mask_rows(start - TAP, TAP, length), mask_rows(start + frames, TAP, length))
    taps = (gain1 * tap0, gain1 * tap2)
    grads = ((f0a_ref, f1a_ref, f2a_ref), (f0z_ref, f1z_ref, f2z_ref))
    his, los = [], []
    for side in range(2):
        f0, f1, f2 = grads[side]
        m = masks[side]
        hi_s, lo_s = [], []
        for s in blocks(width):
            sums = [jnp.zeros((8, LANES), f32)] * 3
            hi_q, lo_q = [], []
            for q in range(0, TAP, SUB):
                at = slice(q, q + SUB)
                hq = h[side * TAP + q : side * TAP + q + SUB, s] + b1[:, s]
                v, t = half_act(hq, a1[:, s], c1[:, s])
                grad = m[at] * (c0[:, s] * f0[0, at, s] - cc[:, s] * f1[0, at, s] - beta[:, s] * f2[0, at, s])
                u = taps[side][:, s] * grad
                gh = u * (d_base[:, s] + d_gain[:, s] * t)
                for k, x_ in enumerate((gh, u * hq, grad * v)):
                    sums[k] = sums[k] + fold(x_)
                hi, lo = split(gh)
                hi_q.append(hi)
                lo_q.append(lo)
            acc[0, :, s] += sums[0]
            acc[1, :, s] += sums[1]
            acc[2 + 2 * side, :, s] += gain1[:, s] * sums[2]
            hi_s.append(jnp.concatenate(hi_q, axis=0))
            lo_s.append(jnp.concatenate(lo_q, axis=0))
        his.append(jnp.concatenate(hi_s, axis=1))
        los.append(jnp.concatenate(lo_s, axis=1))
    hi, lo = jnp.concatenate(his, axis=0), jnp.concatenate(los, axis=0)
    gw[...] += dot0(jnp.concatenate([xhi, xhi, xlo], axis=0), jnp.concatenate([hi, lo, hi], axis=0))
    back = dot(jnp.concatenate([hi, hi, lo], axis=1), wt3[...])
    before_ref[0], after_ref[0] = back[0:TAP], back[TAP:]


def third_kernel(
    rows, len_ref, tm_ref, mine_ref, v_ref, x_ref, f0_ref, f1_ref, f2_ref, gr_ref, z_ref, y_ref,
    ch_ref, bias_ref, w_ref, br_ref, bs_ref, stat, coef, chan, zc, gw0_ref, acc0_ref, *rest
):
    params, rest = rest[: len(PARAMS)], rest[len(PARAMS) :]
    res_ref, skip_ref, gin_ref, keep_ref, send_ref, *rest = rest
    w3, wt, ext, gw, gwt, acc, hb0, hb1, hl0, hl1 = rest
    par = channel(dict(zip(PARAMS, params)))
    i = pl.program_id(0)
    items = ch_ref.shape[0]
    frames, width = v_ref.shape[1:]
    base = gr_ref.shape[2]
    tap0, tap1, tap2 = par("tap0"), par("tap1"), par("tap2")
    a1 = par("slope_in")
    c1 = (1.0 - a1) * (0.5 * LN2)

    @pl.when(i == 0)
    def _():
        w3[...] = stacked3(0.5 * w_ref[...])
        wt[...] = jnp.concatenate(split(w_ref[...].T), axis=1)
        zeros = jnp.zeros((2 * TAP, width), f32)
        ext[0 : 2 * TAP, :] = zeros
        ext[frames + 2 * TAP : frames + 4 * TAP, :] = zeros
        gw[...] = gw0_ref[...]
        gwt[...] = jnp.zeros_like(gwt)
        acc[...] = acc0_ref[...]

    length = len_ref[i]
    start = tm_ref[0] * frames

    def st(k):
        return wide(stat[k, pl.ds(i, 1), :], width)

    scale1, scale2, beta, cut, cut_v = [st(k) for k in range(5)]
    c0, cc = coef[0, pl.ds(i, 1), :], coef[1, pl.ds(i, 1), :]
    gwt[...] += (2.0 * c0) * y_ref[0]
    gain1 = par("gain_in") * scale1
    cut = cut + cut_v * c1
    taps = [gain1 * tap0, gain1 * tap1, gain1 * tap2]
    b1 = 0.5 * par("bias_in")
    d_base, d_gain = 0.5 + 0.5 * a1, 0.5 - 0.5 * a1

    parts = frames // rows
    h_slots, hl_slots = (hb0, hb1), (hl0, hl1)

    def spread(n):
        def multiply(q):
            h_slots[n % 2][q : q + HALF, :] = product3(x_ref[0, n * rows + q : n * rows + q + HALF, :], w3[...])

        return [functools.partial(multiply, q) for q in range(0, rows, HALF)]

    def elementwise(n, masked):
        hb, hl = h_slots[n % 2], hl_slots[n % 2]
        if masked:
            m = mask_rows(start + n * rows, rows, length)

        def unit(s, begin):
            sums = [jnp.zeros((8, LANES), f32)] * 5
            for q in range(begin, begin + HALF, SUB):
                hq = hb[q : q + SUB, s] + b1[:, s]
                r = n * rows + q
                t = jnp.tanh(hq)
                v = v_ref[0, r : r + SUB, s]
                later = ext[r + 3 * TAP : r + 3 * TAP + SUB, s]
                here = ext[r + 2 * TAP : r + 2 * TAP + SUB, s]
                before = ext[r + TAP : r + TAP + SUB, s]
                u = taps[0][:, s] * later + taps[1][:, s] * here + taps[2][:, s] * before
                u = u - cut[:, s] - cut_v[:, s] * v
                vm = v
                if masked:
                    u, vm = u * m[q : q + SUB], v * m[q : q + SUB]
                gh = u * (d_base[:, s] + d_gain[:, s] * t)
                for k, x_ in enumerate((gh, u * hq, later * vm, here * vm, before * vm)):
                    sums[k] = sums[k] + fold(x_)
                hi, lo = split(gh)
                hl[0, q : q + SUB, s] = hi
                hl[1, q : q + SUB, s] = lo
            for k, x_ in enumerate(sums):
                acc[k, :, s] += x_ if k < 2 else gain1[:, s] * x_

        return [functools.partial(unit, s, q) for q in range(0, rows, HALF) for s in blocks(width)]

    def products(n):
        hl = hl_slots[n % 2]

        def weights():
            xhi, xlo = split(x_ref[0, n * rows : (n + 1) * rows, :])
            gw[...] += dot0(jnp.concatenate([xhi, xhi, xlo], axis=0), jnp.concatenate([hl[0], hl[1], hl[0]], axis=0))

        def out(q):
            hi, lo = hl[0, q : q + HALF, :], hl[1, q : q + HALF, :]
            at = slice(n * rows + q, n * rows + q + HALF)
            by_hi = dot(hi, wt[...])
            by_lo = dot(lo, wt[:, 0:base])
            gin_ref[0, at, :] = gr_ref[0, at, :] + (by_hi[:, 0:base] + (by_hi[:, base:] + by_lo))

        return [weights] + [functools.partial(out, q) for q in range(0, rows, HALF)]

    scale_c = stat[1, pl.ds(i, 1), :]
    br, bs = br_ref[...], bs_ref[...]
    zi = zc[pl.ds(i, 1), :]

    def outputs(n, kind):
        at = slice(n * rows, (n + 1) * rows)
        x = x_ref[0, at, :]
        if kind == "none":
            res_ref[0, at, :] = x + br
            skip_ref[0, at, :] = jnp.broadcast_to(bs, (rows, base))
            gin_ref[0, at, :] = gr_ref[0, at, :]
            return
        z = z_ref[0, at, :]
        to_res = scale_c * z[:, 0:base] + zi[:, 0:base]
        to_skip = scale_c * z[:, base:] + zi[:, base:]
        if kind == "some":
            m = mask_rows(start + n * rows, rows, length)
            to_res, to_skip = to_res * m, to_skip * m
        res_ref[0, at, :] = (x + to_res) + br
        skip_ref[0, at, :] = to_skip + bs

    def lift(k):
        for s in blocks(width):
            for q in range(k * rows, (k + 1) * rows, SUB):
                at = slice(q, q + SUB)
                ext[2 * TAP + q : 2 * TAP + q + SUB, s] = (
                    c0[:, s] * f0_ref[0, at, s] - cc[:, s] * f1_ref[0, at, s] - beta[:, s] * f2_ref[0, at, s]
                )

    interleave(spread(0), [functools.partial(lift, k) for k in range(parts)])
    for n in range(parts):
        def step(kind, n=n):
            ahead = spread(n + 1) if n + 1 < parts else []
            if kind == "none":
                for piece in ahead + [functools.partial(outputs, n, kind)]:
                    piece()
                return
            vector = elementwise(n, kind == "some")
            weights, *outs = products(n)
            each = len(vector) // len(outs)
            for j, out in enumerate(outs):
                interleave(ahead[j : j + 1] or [lambda: None], vector[j * each : (j + 1) * each])
                out()
            outputs(n, kind)
            weights()

        t0 = start + n * rows
        full, none = t0 + rows <= length, t0 >= length
        pl.when(full)(functools.partial(step, "full"))
        pl.when(jnp.logical_not(full | none))(functools.partial(step, "some"))
        pl.when(none)(functools.partial(step, "none"))

    @pl.when(i == items - 1)
    def _():
        outer = lax.dot_general(
            ch_ref[:, R_GM, 0 : 2 * base], coef[2], (((0,), (0,)), ((), ())),
            precision=lax.Precision.HIGHEST, preferred_element_type=f32,
        )
        both = (gwt[...] + outer).T
        done = acc[...].sum(axis=1)
        tap_sums = 2.0 * done[2:5]
        by_v = 0.5 * (tap0 * tap_sums[0:1] + tap1 * tap_sums[1:2] + tap2 * tap_sums[2:3])
        slope = (-2.0 / (1.0 - a1)) * (chan[1:2, :] + by_v - done[1:2])
        table = jnp.concatenate([done[0:1], slope, chan[2:4, :], chan[4:7, :] + tap_sums, chan[7:16, :]], axis=0)
        bias = bias_ref[...].sum(axis=0, keepdims=True)
        tail = jnp.concatenate([bias[:, 0:base], bias[:, base:], jnp.zeros((6, base), f32)], axis=0)
        pieces = [both[:, 0:base], both[:, base:]] + [gw[:, s] for s in blocks(width)]
        pieces += [table[:, s] for s in blocks(width)] + [tail]
        half = keep_ref.shape[0]
        pieces.append(jnp.zeros((2 * half - sum(p.shape[0] for p in pieces), LANES), f32))

        def store(first, second):
            at = 0
            for piece in pieces:
                end = at + piece.shape[0]
                for side, ref in enumerate((first, second)):
                    a, b = max(at, side * half), min(end, (side + 1) * half)
                    if a < b:
                        ref[a - side * half : b - side * half, :] = piece[a - at : b - at]
                at = end

        pl.when(mine_ref[0] == 0)(functools.partial(store, keep_ref, send_ref))
        pl.when(mine_ref[0] == 1)(functools.partial(store, send_ref, keep_ref))


def sum_rows(size):
    return -(-size // 256) * 256


def exchange(x, axis):
    return lax.all_to_all(x, axis, 0, 0)


def halves(n_item):
    return [1 << k for k in range(n_item.bit_length() - 1)]


def reduce_all(x, sizes, beside):
    n_tm, n_item = sizes["tm"], sizes["item"]
    keep, send = x

    def swap(y, by):
        return lax.ppermute(y, "item", [(d, d ^ by) for d in range(n_item)])

    for by in halves(n_item):
        if by > 1:
            half = x.shape[0] // 2
            mine = (lax.axis_index("item") // by) % 2
            keep = lax.dynamic_slice_in_dim(x, mine * half, half)
            send = lax.dynamic_slice_in_dim(x, (1 - mine) * half, half)
        x = keep + swap(send, by)
    if n_item == 1:
        x = jnp.concatenate([keep, send])
    parts = exchange(x.reshape((n_tm, x.shape[0] // n_tm) + x.shape[1:]), "tm")
    x = jnp.sum(parts, axis=0)
    x = exchange(jnp.broadcast_to(x[None], (n_tm,) + x.shape), "tm").reshape((-1,) + x.shape[1:])
    for by in halves(n_item)[::-1]:
        if by == 1:
            x, beside = lax.optimization_barrier((x, beside))
        mine = (lax.axis_index("item") // by) % 2
        other = swap(x, by)
        x = jnp.where(mine == 0, jnp.concatenate([x, other]), jnp.concatenate([other, x]))
    return x, beside


def whole(shape):
    return pl.BlockSpec(shape, lambda i: (0,) * len(shape))


def per_item(shape):
    return pl.BlockSpec((1,) + shape, lambda i: (i,) + (0,) * len(shape))


SMEM = pl.BlockSpec(memory_space=pltpu.SMEM)


def body(
    inputs, lengths, counts, weight_in, bias_in, slope_in, gain_in, shift_in, channelwise_taps, channelwise_bias,
    slope_out, gain_out, shift_out, weight_res, bias_res, weight_skip, bias_skip, grad_residual, grad_skip,
):
    items, frames, base = inputs.shape
    width = weight_in.shape[1]
    sources = grad_skip.shape[1]
    tm, across = lax.axis_size("tm"), lax.axis_size("item")
    place = lax.axis_index("tm").astype(jnp.int32).reshape(1)
    mine = (lax.axis_index("item") % 2).astype(jnp.int32).reshape(1)
    up = [(d, d + 1) for d in range(tm - 1)]
    down = [(d + 1, d) for d in range(tm - 1)]
    x_before = lax.ppermute(inputs[:, frames - TAP :], "tm", up)
    x_after = lax.ppermute(inputs[:, :TAP], "tm", down)

    def row(v):
        return v.reshape(1, -1)

    table = [row(bias_in), row(slope_in), row(gain_in), row(shift_in), channelwise_taps, row(channelwise_bias),
             row(slope_out), row(gain_out), row(shift_out)]
    table_specs = [whole(t.shape) for t in table]
    vmem = lambda mib: pltpu.CompilerParams(vmem_limit_bytes=mib * 2**20)

    rows1, rows2, rows3 = (min(c, frames) for c in (CHUNK1, CHUNK2, CHUNK3))
    v1, st1, ch1 = pl.pallas_call(
        functools.partial(first_kernel, rows1),
        grid=(items,),
        in_specs=[SMEM, SMEM, per_item((frames, base)),
                  pl.BlockSpec((1, rows1, base), lambda i: (jnp.minimum(i + 1, items - 1), 0, 0)),
                  whole((base, width)), whole((1, width)), whole((1, width))],
        out_specs=[per_item((frames, width)), whole((tm, items, LANES)), whole((items, 8, width))],
        out_shape=[jax.ShapeDtypeStruct((items, frames, width), f32), jax.ShapeDtypeStruct((tm, items, LANES), f32),
                   jax.ShapeDtypeStruct((items, 8, width), f32)],
        scratch_shapes=[pltpu.VMEM((3 * base, width), bf16), pltpu.VMEM((2, 8, width), f32)]
        + [pltpu.VMEM((rows1, width), f32)] * 2,
        compiler_params=vmem(48),
        name="first",
    )(lengths, place, inputs, inputs, weight_in, table[0], table[1])
    ga1 = exchange(st1, "tm")

    big = jax.ShapeDtypeStruct((items, frames, width), f32)
    f0, f1, f2, z, y, ch, st2, bias = pl.pallas_call(
        functools.partial(second_kernel, rows2),
        grid=(items,),
        in_specs=[SMEM, SMEM, SMEM, per_item((frames, width)), per_item((TAP, base)), per_item((TAP, base)),
                  per_item((frames, base)), per_item((sources, frames, base)), whole((base, width)),
                  whole((width, base)), whole((width, base))] + table_specs + [whole((tm, items, LANES))],
        out_specs=[per_item((frames, width))] * 3 + [per_item((frames, 2 * base)), per_item((2 * base, width)),
                   whole((items, ROWS, width)), whole((tm, items, LANES)), whole((8, 2 * base))],
        out_shape=[big, big, big, jax.ShapeDtypeStruct((items, frames, 2 * base), f32),
                   jax.ShapeDtypeStruct((items, 2 * base, width), f32), jax.ShapeDtypeStruct((items, ROWS, width), f32),
                   jax.ShapeDtypeStruct((tm, items, LANES), f32), jax.ShapeDtypeStruct((8, 2 * base), f32)],
        scratch_shapes=[pltpu.VMEM((3 * base, width), bf16), pltpu.VMEM((6 * base, width), bf16),
                        pltpu.VMEM((3 * width, 2 * base), bf16), pltpu.VMEM((2, items, LANES), f32),
                        pltpu.VMEM((frames + 2 * TAP, width), f32), pltpu.VMEM((ROWS, 8, width), f32),
                        pltpu.VMEM((8, 2 * base), f32), pltpu.VMEM((2 * base, width), f32)]
        + [pltpu.VMEM((rows2, width), f32)] * 2 + [pltpu.VMEM((2, rows2, width), bf16)] * 2
        + [pltpu.VMEM((frames // rows2, 2, rows2, 2 * base), bf16)],
        compiler_params=vmem(48),
        name="second",
    )(lengths, counts, place, v1, x_before, x_after, grad_residual, grad_skip, weight_in, weight_res, weight_skip,
      *table, ga1)
    ga2 = exchange(st2, "tm")

    n_sum = sum_rows(2 * width + 4 * base + 64 + 8)
    out = jax.ShapeDtypeStruct((items, frames, base), f32)
    strip = lambda k: pl.BlockSpec((1, TAP, width), lambda i: (i, k, 0))
    last = frames // TAP - 1
    small = [((5, items, LANES), f32), ((3, items, width), f32), ((16, width), f32), ((items, 2 * base), f32),
             ((base, width), f32), ((8, 8, width), f32)]
    to_last, to_next, *given = pl.pallas_call(
        functools.partial(edge_kernel, frames),
        grid=(items,),
        in_specs=[SMEM, SMEM, per_item((TAP, base)), per_item((TAP, base))] + [strip(0), strip(last)] * 3
        + [whole((items, 8, width)), whole((items, ROWS, width)), whole((base, width)), whole((width, base)),
           whole((width, base))] + table_specs + [whole((tm, items, LANES))] * 2,
        out_specs=[per_item((TAP, base))] * 2 + [whole(shape) for shape, _ in small],
        out_shape=[jax.ShapeDtypeStruct((items, TAP, base), f32)] * 2
        + [jax.ShapeDtypeStruct(shape, dtype) for shape, dtype in small],
        scratch_shapes=[pltpu.VMEM((3 * base, width), bf16), pltpu.VMEM((3 * width, base), bf16)],
        compiler_params=vmem(48),
        name="edge",
    )(lengths, place, x_before, x_after, f0, f0, f1, f1, f2, f2, ch1, ch, weight_in, weight_res, weight_skip, *table,
      ga1, ga2)
    from_next = lax.ppermute(to_last, "tm", down)
    from_last = lax.ppermute(to_next, "tm", up)

    res, skip, gin, *sums = pl.pallas_call(
        functools.partial(third_kernel, rows3),
        grid=(items,),
        in_specs=[SMEM, SMEM, SMEM, per_item((frames, width)), per_item((frames, base)), per_item((frames, width)),
                  per_item((frames, width)), per_item((frames, width)), per_item((frames, base)),
                  per_item((frames, 2 * base)), per_item((2 * base, width)), whole((items, ROWS, width)),
                  whole((8, 2 * base)), whole((base, width)), whole((1, base)), whole((1, base))]
        + [whole(shape) for shape, _ in small] + table_specs,
        out_specs=[per_item((frames, base))] * 3 + [whole((n_sum // 2, base))] * 2,
        out_shape=[out, out, out] + [jax.ShapeDtypeStruct((n_sum // 2, base), f32)] * 2,
        scratch_shapes=[pltpu.VMEM((3 * base, width), bf16), pltpu.VMEM((width, 2 * base), bf16),
                        pltpu.VMEM((frames + 4 * TAP, width), f32),
                        pltpu.VMEM((base, width), f32), pltpu.VMEM((2 * base, width), f32),
                        pltpu.VMEM((8, 8, width), f32)]
        + [pltpu.VMEM((rows3, width), f32)] * 2 + [pltpu.VMEM((2, rows3, width), bf16)] * 2,
        compiler_params=vmem(48),
        cost_estimate=pl.CostEstimate(flops=items * frames * width * base * 30, transcendentals=items * frames * width,
                                      bytes_accessed=items * frames * (5 * width + 7 * base) * 4),
        name="third",
    )(lengths, place, mine, v1, inputs, f0, f1, f2, grad_residual, z, y, ch, bias, weight_in, row(bias_res), row(bias_skip),
      *given, *table)

    sums, from_next, from_last = lax.optimization_barrier((sums, from_next, from_last))
    gin = gin.at[:, frames - TAP :].add(from_next)
    gin = gin.at[:, :TAP].add(from_last)
    total, gin = reduce_all(sums, {"tm": tm, "item": across}, gin)

    g_res, g_skip = total[0:width], total[width : 2 * width]
    at0 = 2 * width + 4 * base
    g_in = total[2 * width : at0].reshape(4, base, LANES).transpose(1, 0, 2).reshape(base, width)
    vec = total[at0 : at0 + 64].reshape(4, 16, LANES).transpose(1, 0, 2).reshape(16, width)
    return (
        res, skip, gin, g_in, vec[0], vec[1], vec[2], vec[3], vec[4:7], vec[7], vec[8], vec[9], vec[10],
        g_res, total[at0 + 64], g_skip, total[at0 + 65],
    )


def solution(mesh):
    spread = P("item", "tm", None)
    return jax.shard_map(
        body,
        mesh=mesh,
        in_specs=(spread, P("item"), P("item")) + (P(),) * 14 + (spread, P("item", None, "tm", None)),
        out_specs=(spread,) * 3 + (P(),) * 14,
        check_vma=False,
    )
```

```python
import functools

import jax
import jax.numpy as jnp
from jax import lax
from jax.experimental import pallas as pl
from jax.experimental.pallas import tpu as pltpu
from jax.sharding import PartitionSpec as P

TAP = 128
LANES = 128
EPSILON = 1e-05
LN2 = 0.6931471805599453
f32 = jnp.float32
bf16 = jnp.bfloat16

PARAMS = ("bias_in", "slope_in", "gain_in", "shift_in", "taps", "bias_dw", "slope_out", "gain_out", "shift_out")
(R_P, R_S, R_SS, R_GD, R_GS, R_H0, R_H1, R_H2, R_HF0, R_HF1, R_HF2, R_PF0, R_PF1, R_PF2,
 R_A0, R_A1, R_A2, R_Z0, R_Z1, R_Z2, R_GM) = range(21)
ROWS = 24
SUB = 32
HALF = 128
CHUNK1, CHUNK2, CHUNK3 = 256, 256, 256


def split(x):
    hi = x.astype(bf16)
    lo = (x - hi.astype(f32)).astype(bf16)
    return hi, lo


def dot(a, b):
    return jnp.dot(a, b, preferred_element_type=f32)


def dot0(a, b):
    return lax.dot_general(a, b, (((0,), (0,)), ((), ())), preferred_element_type=f32)


def product3(x, w3):
    hi, lo = split(x)
    return dot(jnp.concatenate([hi, hi, lo], axis=1), w3)


def stacked3(w):
    hi, lo = split(w)
    return jnp.concatenate([hi, lo, hi], axis=0)


def half_act(h, a, c):
    t = jnp.tanh(h)
    return jnp.maximum(h, a * h) - c * jnp.log2(1.0 + jnp.abs(t)), t


def fold(x):
    rows, cols = x.shape
    return x.reshape(rows // 8, 8, cols).sum(axis=0)


def mask_rows(first, rows, length):
    row = lax.broadcasted_iota(jnp.int32, (rows, 1), 0) + first
    return ((row >= 0) & (row < length)).astype(f32)


def lane_put(values):
    shape = values[0].shape[:-1] + (LANES,)
    lane = lax.broadcasted_iota(jnp.int32, shape, len(shape) - 1)
    out = jnp.zeros(shape, f32)
    for k, v in enumerate(values):
        out = jnp.where(lane == k, jnp.broadcast_to(v, shape), out)
    return out


def channel(ref):
    def get(name):
        if name.startswith("tap"):
            k = int(name[3])
            return ref["taps"][k : k + 1]
        return ref[name][...]

    return get


def interleave(first, second):
    done = 0
    for n, piece in enumerate(first):
        piece()
        upto = (n + 1) * len(second) // len(first)
        for other in second[done:upto]:
            other()
        done = upto
    for other in second[done:]:
        other()


def blocks(width):
    return [slice(j * LANES, (j + 1) * LANES) for j in range(width // LANES)]


def per_item_column(values):
    row = lax.broadcasted_iota(jnp.int32, (len(values), 1), 0)
    out = jnp.zeros((len(values), 1), f32)
    for k, v in enumerate(values):
        out = jnp.where(row == k, v, out)
    return out


def frames_here(len_ref, start, frames, items):
    return per_item_column([jnp.clip(len_ref[k] - start, 0, frames).astype(f32) for k in range(items)])


def first_kernel(rows, len_ref, tm_ref, x_ref, xn_ref, w_ref, b_ref, a_ref, v_ref, st_ref, ch_ref, w3, acc, hb0, hb1):
    i = pl.program_id(0)
    items = ch_ref.shape[0]
    frames, width = v_ref.shape[1:]
    slots = (hb0, hb1)

    @pl.when(i == 0)
    def _():
        w3[...] = stacked3(0.5 * w_ref[...])
        hb0[...] = product3(x_ref[0, 0:rows, :], w3[...])

    length = len_ref[i]
    start = tm_ref[0] * frames
    b, a = 0.5 * b_ref[...], a_ref[...]
    c = (1.0 - a) * (0.5 * LN2)
    centre = half_act(hb0[0:8, :] + b, a, c)[0][0:1]
    parts = frames // rows

    for k in range(parts):
        def step(masked, k=k):
            h, then = slots[k % 2], slots[(k + 1) % 2]
            if masked:
                m = mask_rows(start + k * rows, rows, length)

            def ahead(q):
                x = x_ref[0, (k + 1) * rows + q : (k + 1) * rows + q + HALF, :] if k < parts - 1 else xn_ref[0, q : q + HALF, :]
                then[q : q + HALF, :] = product3(x, w3[...])

            def unit(s):
                total = square = jnp.zeros((8, LANES), f32)
                for q in range(0, rows, SUB):
                    v, _ = half_act(h[q : q + SUB, s] + b[:, s], a[:, s], c[:, s])
                    v_ref[0, k * rows + q : k * rows + q + SUB, s] = v
                    d = v - centre[:, s]
                    dm = d * m[q : q + SUB] if masked else d
                    total = total + fold(dm)
                    square = square + fold(dm * d)
                acc[0, :, s] = total if k == 0 else acc[0, :, s] + total
                acc[1, :, s] = square if k == 0 else acc[1, :, s] + square

            interleave([functools.partial(ahead, q) for q in range(0, rows, HALF)],
                       [functools.partial(unit, s) for s in blocks(width)])

        full = start + (k + 1) * rows <= length
        pl.when(full)(functools.partial(step, False))
        pl.when(jnp.logical_not(full))(functools.partial(step, True))

    ch_ref[pl.ds(i, 1), 0, :] = acc[0].sum(axis=0, keepdims=True)
    ch_ref[pl.ds(i, 1), 1, :] = acc[1].sum(axis=0, keepdims=True)
    ch_ref[pl.ds(i, 1), 2, :] = centre

    @pl.when(i == items - 1)
    def _():
        n = frames_here(len_ref, start, frames, items)
        safe = jnp.maximum(n, 1.0)
        total, square, centre = ch_ref[:, 0, :], ch_ref[:, 1, :], ch_ref[:, 2, :]
        ch_ref[:, 0, :] = total + n * centre
        ch_ref[:, 1, :] = square + 2.0 * centre * total + n * centre * centre
        total = total / safe
        level = centre + c + total
        mean = level.sum(axis=1, keepdims=True) / width
        dev = level - mean
        spread = (square - safe * total * total + safe * dev * dev).sum(axis=1, keepdims=True)
        some = (n > 0).astype(f32)
        st_ref[...] = jnp.broadcast_to(lane_put([2.0 * mean * some, 4.0 * spread * some, n])[None], st_ref.shape)


def merged(gathered, width):
    mean_d, spread_d, n_d = gathered[:, :, 0:1], gathered[:, :, 1:2], gathered[:, :, 2:3]
    n = n_d.sum(axis=0)
    mean = (n_d * mean_d).sum(axis=0) / n
    dev = mean_d - mean[None]
    spread = (spread_d + n_d * width * dev * dev).sum(axis=0)
    count = n * width
    return mean, lax.rsqrt(spread / count + EPSILON), count


def wide(x, width):
    return jnp.broadcast_to(x[:, 0:1], (x.shape[0], width))


def second_kernel(
    rows, len_ref, cnt_ref, tm_ref, v_ref, xb_ref, xa_ref, gr_ref, gk_ref, w_ref, wr_ref, ws_ref, *rest
):
    params, rest = rest[: len(PARAMS)], rest[len(PARAMS) :]
    ga_ref, f0_ref, f1_ref, d_ref, y_ref, ch_ref, st_ref, bias_ref, *rest = rest
    w3, wt3, stat, fst, acc, gacc, yacc, gs0, gs1, hl0, hl1, gb = rest
    par = channel(dict(zip(PARAMS, params)))
    i = pl.program_id(0)
    items = ch_ref.shape[0]
    frames, width = v_ref.shape[1:]
    base = gr_ref.shape[2]
    parts = frames // rows
    gs_slots, hl_slots = (gs0, gs1), (hl0, hl1)

    @pl.when(i == 0)
    def _():
        w3[...] = stacked3(0.5 * w_ref[...])
        both = jnp.concatenate([wr_ref[...], ws_ref[...]], axis=1)
        wt3[...] = stacked3(both.T)
        mean, scale, _ = merged(ga_ref[...], width)
        stat[0] = jnp.broadcast_to(mean, stat.shape[1:])
        stat[1] = jnp.broadcast_to(scale, stat.shape[1:])
        bias_ref[...] = jnp.zeros_like(bias_ref)
        ch_ref[...] = jnp.zeros_like(ch_ref)

    length = len_ref[i]
    start = tm_ref[0] * frames
    mean = wide(stat[0, pl.ds(i, 1), :], width)
    scale = wide(stat[1, pl.ds(i, 1), :], width)
    a1 = par("slope_in")
    c1 = (1.0 - a1) * (0.5 * LN2)
    gain = 2.0 * par("gain_in") * scale
    shift = par("shift_in") + gain * (c1 - 0.5 * mean)
    b1 = 0.5 * par("bias_in")
    alive = [(s < cnt_ref[i]).astype(f32) for s in range(gk_ref.shape[1])]
    taps = [0.5 * par(f"tap{k}") for k in range(3)]
    bias = 0.5 * par("bias_dw")
    a2 = par("slope_out")
    c2 = (1.0 - a2) * (0.5 * LN2)
    d_base, d_gain = 0.5 + 0.5 * a2, 0.5 - 0.5 * a2

    def cotangents(k):
        at = slice(k * rows, (k + 1) * rows)
        g_res = gr_ref[0, at, :]
        g_skip = alive[0] * gk_ref[0, 0, at, :]
        for s in range(1, len(alive)):
            g_skip = g_skip + alive[s] * gk_ref[0, s, at, :]
        return jnp.concatenate([g_res, g_skip], axis=1)

    def spread(k):
        def prepare():
            both = cotangents(k)
            bias_ref[...] += fold(both)
            row = lax.broadcasted_iota(jnp.int32, (rows, 1), 0)
            both = jnp.where(row < length - start - k * rows, both, 0.0)
            gacc[...] = fold(both) if k == 0 else gacc[...] + fold(both)
            ghi, glo = split(both)
            gb[k, 0], gb[k, 1] = ghi, glo

        def multiply(q):
            if q == 0:
                prepare()
            ghi, glo = gb[k, 0, q : q + HALF, :], gb[k, 1, q : q + HALF, :]
            gs_slots[k % 2][q : q + HALF, :] = dot(jnp.concatenate([ghi, ghi, glo], axis=1), wt3[...])

        return [functools.partial(multiply, q) for q in range(0, rows, HALF)]

    def products(k):
        hl = hl_slots[k % 2]

        def weights(q):
            at = slice(q, q + base)
            ghi, glo = gb[k, 0, :, at], gb[k, 1, :, at]
            y = dot0(jnp.concatenate([ghi, ghi, glo], axis=0), jnp.concatenate([hl[0], hl[1], hl[0]], axis=0))
            if k == parts - 1:
                y_ref[0, at, :] = yacc[at, :] + y if k else y
            else:
                yacc[at, :] = yacc[at, :] + y if k else y

        return [functools.partial(weights, q) for q in (0, base)]

    h = product3(jnp.concatenate([xb_ref[0], xa_ref[0]], axis=0), w3[...])
    for piece in spread(0):
        piece()
    for side, at in ((0, 0), (1, frames + TAP)):
        m = mask_rows(start + at - TAP, TAP, length)
        for s in blocks(width):
            for q in range(0, TAP, SUB):
                v, _ = half_act(h[side * TAP + q : side * TAP + q + SUB, s] + b1[:, s], a1[:, s], c1[:, s])
                fst[at + q : at + q + SUB, s] = m[q : q + SUB] * (gain[:, s] * v + shift[:, s])

    def lift(k, _):
        r0 = pl.multiple_of(k * TAP, TAP)
        full = start + r0 + TAP <= length

        @pl.when(full)
        def _():
            fst[pl.ds(TAP + r0, TAP), :] = gain * v_ref[0, pl.ds(r0, TAP), :] + shift

        @pl.when(jnp.logical_not(full))
        def _():
            m = mask_rows(start + r0, TAP, length)
            fst[pl.ds(TAP + r0, TAP), :] = m * (gain * v_ref[0, pl.ds(r0, TAP), :] + shift)

        return 0

    lax.fori_loop(0, frames // TAP, lift, 0)

    def halved(r, size, s):
        return (
            taps[0][:, s] * fst[r : r + size, s]
            + taps[1][:, s] * fst[r + TAP : r + TAP + size, s]
            + taps[2][:, s] * fst[r + 2 * TAP : r + 2 * TAP + size, s]
            + bias[:, s]
        )

    point = jnp.concatenate(
        [half_act(halved(0, 8, s), a2[:, s], c2[:, s])[0][0:1] for s in blocks(width)], axis=1
    )
    tracked = [r for r in range(R_S, R_A0) if r != R_GS]

    def elementwise(k, masked):
        gs, hl = gs_slots[k % 2], hl_slots[k % 2]
        if masked:
            m = mask_rows(start + k * rows, rows, length)

        def unit(s, begin):
            zero = jnp.zeros((8, LANES), f32)
            sums = {r: zero for r in tracked}
            for q in range(begin, begin + HALF, SUB):
                at = slice(k * rows + q, k * rows + q + SUB)
                f = halved(k * rows + q, SUB, s)
                v, t = half_act(f, a2[:, s], c2[:, s])
                dm = d_base[:, s] + d_gain[:, s] * t
                d = v - point[:, s]
                g = gs[q : q + SUB, s]
                dd, fm = d, f
                if masked:
                    mq = m[q : q + SUB]
                    dm, dd, fm = dm * mq, d * mq, f * mq
                f0 = g * dm
                f2 = d * dm
                f0_ref[0, at, s] = f0
                f1_ref[0, at, s] = dm
                d_ref[0, at, s] = d
                for r, x in (
                    (R_S, dd), (R_SS, dd * d), (R_GD, g * d), (R_H0, f0), (R_H1, dm), (R_H2, f2), (R_HF0, f0 * f),
                    (R_HF1, dm * f), (R_HF2, f2 * f), (R_PF0, g * f), (R_PF1, fm), (R_PF2, dd * f),
                ):
                    sums[r] = sums[r] + fold(x)
                hi, lo = split(d)
                hl[0, q : q + SUB, s] = hi
                hl[1, q : q + SUB, s] = lo
            for r, x in sums.items():
                acc[r, :, s] = x if k == 0 and begin == 0 else acc[r, :, s] + x

        return [functools.partial(unit, s, q) for q in range(0, rows, HALF) for s in blocks(width)]

    def nothing(k):
        at = slice(k * rows, (k + 1) * rows)
        zero = jnp.zeros((rows, width), f32)
        for ref in (f0_ref, f1_ref, d_ref):
            ref[0, at, :] = zero
        hl_slots[k % 2][...] = jnp.zeros_like(hl0)
        if k == 0:
            for r in tracked:
                acc[r] = jnp.zeros((8, width), f32)

    for k in range(parts):
        def step(kind, k=k):
            matrix = (spread(k + 1) if k + 1 < parts else []) + (products(k - 1) if k > 0 else [])
            interleave(matrix, [functools.partial(nothing, k)] if kind == "none" else elementwise(k, kind == "some"))

        t0 = start + k * rows
        full, none = t0 + rows <= length, t0 >= length
        pl.when(full)(functools.partial(step, "full"))
        pl.when(jnp.logical_not(full | none))(functools.partial(step, "some"))
        pl.when(none)(functools.partial(step, "none"))
    for piece in products(parts - 1):
        piece()

    edges = acc.at[pl.ds(R_A0, 6)]
    edges[...] = jnp.zeros(edges.shape, f32)

    def edge(k, _):
        r0 = pl.multiple_of(k * TAP, TAP)
        t0 = start + r0
        for row, near in ((R_A0, t0 < TAP), (R_Z0, (t0 < length) & (t0 + TAP > length - TAP))):
            @pl.when(near)
            def _():
                at = lax.broadcasted_iota(jnp.int32, (TAP, 1), 0) + t0
                there = ((at < TAP) if row == R_A0 else (at >= length - TAP)).astype(f32)
                f1 = there * f1_ref[0, pl.ds(r0, TAP), :]
                acc[row] += fold(there * f0_ref[0, pl.ds(r0, TAP), :])
                acc[row + 1] += fold(f1)
                acc[row + 2] += fold(f1 * d_ref[0, pl.ds(r0, TAP), :])
        return 0

    lax.fori_loop(0, frames // TAP, edge, 0)

    ch_ref[pl.ds(i, 1), R_GM, 0 : 2 * base] = gacc[...].sum(axis=0, keepdims=True)
    ch_ref[pl.ds(i, 1), R_P, :] = 2.0 * (point + c2)
    for r in range(R_S, R_GM):
        if r != R_GS:
            total = acc[r].sum(axis=0, keepdims=True)
            if r in (R_S, R_GD, R_H2, R_HF0, R_HF1, R_PF0, R_PF1, R_A2, R_Z2):
                total = 2.0 * total
            if r in (R_SS, R_HF2, R_PF2):
                total = 4.0 * total
            ch_ref[pl.ds(i, 1), r, :] = total

    @pl.when(i == items - 1)
    def _():
        gm = jnp.concatenate([ch_ref[:, R_GM, 0 : 2 * base]] * 2, axis=0)
        ch_ref[:, R_GS, :] = product3(gm, wt3[...])[0:items]

        def got(r):
            return ch_ref[:, r, :]

        n = frames_here(len_ref, start, frames, items)
        some = (n > 0).astype(f32)
        safe = jnp.maximum(n, 1.0)
        point, offset = got(R_P), got(R_S) / safe
        level = point + offset
        mean2 = level.sum(axis=1, keepdims=True) / width
        dev = level - mean2
        spread2 = (got(R_SS) - safe * offset * offset + safe * dev * dev).sum(axis=1, keepdims=True)
        point = point - mean2
        gout = par("gain_out")
        tap0, tap1, tap2 = par("tap0"), par("tap1"), par("tap2")
        g1, sh1, cb = par("gain_in"), par("shift_in"), par("bias_dw")

        def summed(x):
            return x.sum(axis=1, keepdims=True)

        s1 = summed(gout * got(R_GS))
        s2 = summed(gout * (got(R_GD) + point * got(R_GS)))
        t1, t2 = [], []
        for q in range(3):
            h, hf, h_a, h_z = got(R_H0 + q), got(R_HF0 + q), got(R_A0 + q), got(R_Z0 + q)
            if q == 0:
                h, hf, h_a, h_z = gout * h, gout * hf, gout * h_a, gout * h_z
            if q == 2:
                h, hf = h + point * got(R_H1), hf + point * got(R_HF1)
                h_a, h_z = h_a + point * got(R_A1), h_z + point * got(R_Z1)
            kh = (tap0 + tap1 + tap2) * h - tap0 * h_a - tap2 * h_z
            t1.append(summed(g1 * kh))
            t2.append(summed(hf - cb * h - sh1 * kh))
        row = lane_put([mean2 * some, spread2 * some, n, s1, s2] + t1 + t2)
        st_ref[...] = jnp.broadcast_to(row[None], st_ref.shape)


def edge_kernel(
    frames, len_ref, tm_ref, xb_ref, xa_ref, f0a_ref, f0z_ref, f1a_ref, f1z_ref, da_ref, dz_ref,
    ch1_ref, ch_ref, w_ref, wr_ref, ws_ref, *rest
):
    params, rest = rest[: len(PARAMS)], rest[len(PARAMS) :]
    ga1_ref, ga2_ref, before_ref, after_ref, stat_ref, coef_ref, chan_ref, zc_ref, gw, acc, w3, wt3 = rest
    par = channel(dict(zip(PARAMS, params)))
    i = pl.program_id(0)
    width = f0a_ref.shape[2]
    tap0, tap1, tap2 = par("tap0"), par("tap1"), par("tap2")
    a1 = par("slope_in")
    c1 = (1.0 - a1) * (0.5 * LN2)

    def put(k, x):
        stat_ref[k] = jnp.broadcast_to(x, stat_ref.shape[1:])

    @pl.when(i == 0)
    def _():
        w3[...] = stacked3(0.5 * w_ref[...])
        wt3[...] = stacked3(w_ref[...].T)
        mean1, scale1, count = merged(ga1_ref[...], width)
        mean2, scale2, _ = merged(ga2_ref[...], width)
        g = ga2_ref[...]

        def lane(k):
            return g[:, :, k : k + 1]

        dev = lane(0) - mean2[None]
        s1 = lane(3).sum(axis=0)
        s2 = (lane(4) + dev * lane(3)).sum(axis=0)
        alpha = scale2 * s1 / count
        beta = scale2 * scale2 * scale2 * s2 / count
        t1 = scale2 * lane(5).sum(axis=0) - alpha * lane(6).sum(axis=0) - beta * (lane(7) + dev * lane(6)).sum(axis=0)
        t2 = scale2 * lane(8).sum(axis=0) - alpha * lane(9).sum(axis=0) - beta * (lane(10) + dev * lane(9)).sum(axis=0)
        cut = scale1 * t1 / count
        cut_v = scale1 * scale1 * t2 / count
        put(0, scale1)
        put(1, scale2)
        put(2, 2.0 * beta)
        put(3, cut - cut_v * mean1)
        put(4, 2.0 * cut_v)
        delta = ch_ref[:, R_P, :] - mean2
        coef_ref[0] = scale2 * par("gain_out")
        coef_ref[1] = alpha + beta * delta
        coef_ref[2] = scale2 * par("gain_out") * delta + par("shift_out")
        both = jnp.concatenate([wr_ref[...], ws_ref[...]], axis=1)
        zc_ref[...] = lax.dot_general(
            coef_ref[2], both, (((1,), (0,)), ((), ())), precision=lax.Precision.HIGHEST, preferred_element_type=f32
        )

        def row(r):
            return ch_ref[:, r, :]

        c0, cc = coef_ref[0], coef_ref[1]

        def comb(r):
            return c0 * row(r) - cc * row(r + 1) - beta * row(r + 2)

        h, hf, h_a, h_z = comb(R_H0), comb(R_HF0), comb(R_A0), comb(R_Z0)
        kh = (tap0 + tap1 + tap2) * h - tap0 * h_a - tap2 * h_z
        n = ga2_ref[pl.ds(tm_ref[0], 1), :, 2:3][0]
        total = c0 * row(R_GS) - cc * n - beta * row(R_S)
        total_d = c0 * row(R_GD) - cc * row(R_S) - beta * row(R_SS)
        total_f = c0 * row(R_PF0) - cc * row(R_PF1) - beta * row(R_PF2)
        slope = (total_d + row(R_P) * total - total_f) / (1.0 - par("slope_out"))

        def over(x):
            return x.sum(axis=0, keepdims=True)

        gain_out = over(scale2 * row(R_GD) + (scale2 * delta) * row(R_GS))
        gain_in = over(hf - par("bias_dw") * h - par("shift_in") * kh) / par("gain_in")
        gain1 = par("gain_in") * scale1
        shift = par("shift_in") + gain1 * (2.0 * c1 - mean1)
        m1, m2 = ch1_ref[:, 0, :], ch1_ref[:, 1, :]
        k0 = cut - cut_v * mean1 + 2.0 * cut_v * c1
        k1 = 2.0 * cut_v
        act_sum = gain1 * kh - k0 * n - k1 * m1
        act_v = -(k0 * m1 + k1 * m2)
        zero = jnp.zeros((1, width), f32)
        chan_ref[...] = jnp.concatenate(
            [zero, over(c1 * act_sum + act_v), gain_in, over(kh), over(shift * (h - h_a)), over(shift * h),
             over(shift * (h - h_z)), over(h), -over(slope), gain_out, over(row(R_GS)), jnp.zeros((5, width), f32)],
            axis=0,
        )
        gw[...] = jnp.zeros_like(gw)
        acc[...] = jnp.zeros_like(acc)

    length = len_ref[i]
    start = tm_ref[0] * frames

    def st(k):
        return wide(stat_ref[k, pl.ds(i, 1), :], width)

    gain1, beta = par("gain_in") * st(0), st(2)
    c0, cc = coef_ref[0, pl.ds(i, 1), :], coef_ref[1, pl.ds(i, 1), :]
    b1 = 0.5 * par("bias_in")
    d_base, d_gain = 0.5 + 0.5 * a1, 0.5 - 0.5 * a1
    x = jnp.concatenate([xb_ref[0], xa_ref[0]], axis=0)
    xhi, xlo = split(x)
    h = dot(jnp.concatenate([xhi, xhi, xlo], axis=1), w3[...])
    masks = (mask_rows(start - TAP, TAP, length), mask_rows(start + frames, TAP, length))
    taps = (gain1 * tap0, gain1 * tap2)
    grads = ((f0a_ref, f1a_ref, da_ref), (f0z_ref, f1z_ref, dz_ref))
    his, los = [], []
    for side in range(2):
        f0, f1, d = grads[side]
        m = masks[side]
        hi_s, lo_s = [], []
        for s in blocks(width):
            sums = [jnp.zeros((8, LANES), f32)] * 3
            hi_q, lo_q = [], []
            for q in range(0, TAP, SUB):
                at = slice(q, q + SUB)
                hq = h[side * TAP + q : side * TAP + q + SUB, s] + b1[:, s]
                v, t = half_act(hq, a1[:, s], c1[:, s])
                grad = m[at] * (c0[:, s] * f0[0, at, s] - f1[0, at, s] * (cc[:, s] + beta[:, s] * d[0, at, s]))
                u = taps[side][:, s] * grad
                gh = u * (d_base[:, s] + d_gain[:, s] * t)
                for k, x_ in enumerate((gh, u * hq, grad * v)):
                    sums[k] = sums[k] + fold(x_)
                hi, lo = split(gh)
                hi_q.append(hi)
                lo_q.append(lo)
            acc[0, :, s] += sums[0]
            acc[1, :, s] += sums[1]
            acc[2 + 2 * side, :, s] += gain1[:, s] * sums[2]
            hi_s.append(jnp.concatenate(hi_q, axis=0))
            lo_s.append(jnp.concatenate(lo_q, axis=0))
        his.append(jnp.concatenate(hi_s, axis=1))
        los.append(jnp.concatenate(lo_s, axis=1))
    hi, lo = jnp.concatenate(his, axis=0), jnp.concatenate(los, axis=0)
    gw[...] += dot0(jnp.concatenate([xhi, xhi, xlo], axis=0), jnp.concatenate([hi, lo, hi], axis=0))
    back = dot(jnp.concatenate([hi, hi, lo], axis=1), wt3[...])
    before_ref[0], after_ref[0] = back[0:TAP], back[TAP:]


def third_kernel(
    rows, len_ref, tm_ref, mine_ref, v_ref, x_ref, f0_ref, f1_ref, d_ref, gr_ref, y_ref,
    ch_ref, bias_ref, w_ref, wr_ref, ws_ref, br_ref, bs_ref, stat, coef, chan, zc, gw0_ref, acc0_ref, *rest
):
    params, rest = rest[: len(PARAMS)], rest[len(PARAMS) :]
    res_ref, skip_ref, gin_ref, keep_ref, send_ref, *rest = rest
    w3, wt, wg3, ext, gw, gwt, acc, hb0, hb1, hl0, hl1 = rest
    par = channel(dict(zip(PARAMS, params)))
    i = pl.program_id(0)
    items = ch_ref.shape[0]
    frames, width = v_ref.shape[1:]
    base = gr_ref.shape[2]
    tap0, tap1, tap2 = par("tap0"), par("tap1"), par("tap2")
    a1 = par("slope_in")
    c1 = (1.0 - a1) * (0.5 * LN2)

    @pl.when(i == 0)
    def _():
        w3[...] = stacked3(0.5 * w_ref[...])
        wt[...] = jnp.concatenate(split(w_ref[...].T), axis=1)
        both = jnp.concatenate([wr_ref[...], ws_ref[...]], axis=1)
        wg3[...] = stacked3((both.T * (2.0 * par("gain_out"))).T)
        zeros = jnp.zeros((2 * TAP, width), f32)
        ext[0 : 2 * TAP, :] = zeros
        ext[frames + 2 * TAP : frames + 4 * TAP, :] = zeros
        gw[...] = gw0_ref[...]
        gwt[...] = jnp.zeros_like(gwt)
        acc[...] = acc0_ref[...]

    length = len_ref[i]
    start = tm_ref[0] * frames

    def st(k):
        return wide(stat[k, pl.ds(i, 1), :], width)

    scale1, scale2, beta, cut, cut_v = [st(k) for k in range(5)]
    c0, cc = coef[0, pl.ds(i, 1), :], coef[1, pl.ds(i, 1), :]
    gwt[...] += (2.0 * c0) * y_ref[0]
    gain1 = par("gain_in") * scale1
    cut = cut + cut_v * c1
    taps = [gain1 * tap0, gain1 * tap1, gain1 * tap2]
    b1 = 0.5 * par("bias_in")
    d_base, d_gain = 0.5 + 0.5 * a1, 0.5 - 0.5 * a1

    parts = frames // rows
    h_slots, hl_slots = (hb0, hb1), (hl0, hl1)

    def spread(n):
        def multiply(q):
            h_slots[n % 2][q : q + HALF, :] = product3(x_ref[0, n * rows + q : n * rows + q + HALF, :], w3[...])

        return [functools.partial(multiply, q) for q in range(0, rows, HALF)]

    def elementwise(n, masked):
        hb, hl = h_slots[n % 2], hl_slots[n % 2]
        if masked:
            m = mask_rows(start + n * rows, rows, length)

        def unit(s, begin):
            sums = [jnp.zeros((8, LANES), f32)] * 5
            for q in range(begin, begin + HALF, SUB):
                hq = hb[q : q + SUB, s] + b1[:, s]
                r = n * rows + q
                t = jnp.tanh(hq)
                v = v_ref[0, r : r + SUB, s]
                later = ext[r + 3 * TAP : r + 3 * TAP + SUB, s]
                here = ext[r + 2 * TAP : r + 2 * TAP + SUB, s]
                before = ext[r + TAP : r + TAP + SUB, s]
                u = taps[0][:, s] * later + taps[1][:, s] * here + taps[2][:, s] * before
                u = u - cut[:, s] - cut_v[:, s] * v
                vm = v
                if masked:
                    u, vm = u * m[q : q + SUB], v * m[q : q + SUB]
                gh = u * (d_base[:, s] + d_gain[:, s] * t)
                for k, x_ in enumerate((gh, u * hq, later * vm, here * vm, before * vm)):
                    sums[k] = sums[k] + fold(x_)
                hi, lo = split(gh)
                hl[0, q : q + SUB, s] = hi
                hl[1, q : q + SUB, s] = lo
            for k, x_ in enumerate(sums):
                acc[k, :, s] += x_ if k < 2 else gain1[:, s] * x_

        return [functools.partial(unit, s, q) for q in range(0, rows, HALF) for s in blocks(width)]

    def products(n):
        hl = hl_slots[n % 2]

        def weights():
            xhi, xlo = split(x_ref[0, n * rows : (n + 1) * rows, :])
            gw[...] += dot0(jnp.concatenate([xhi, xhi, xlo], axis=0), jnp.concatenate([hl[0], hl[1], hl[0]], axis=0))

        def out(q):
            hi, lo = hl[0, q : q + HALF, :], hl[1, q : q + HALF, :]
            at = slice(n * rows + q, n * rows + q + HALF)
            by_hi = dot(hi, wt[...])
            by_lo = dot(lo, wt[:, 0:base])
            gin_ref[0, at, :] = gr_ref[0, at, :] + (by_hi[:, 0:base] + (by_hi[:, base:] + by_lo))

        return [weights] + [functools.partial(out, q) for q in range(0, rows, HALF)]

    scale_c = stat[1, pl.ds(i, 1), :]
    br, bs = br_ref[...], bs_ref[...]
    zi = zc[pl.ds(i, 1), :]

    def outputs(n, kind, q):
        at = slice(n * rows + q, n * rows + q + HALF)
        x = x_ref[0, at, :]
        if kind == "none":
            res_ref[0, at, :] = x + br
            skip_ref[0, at, :] = jnp.broadcast_to(bs, (HALF, base))
            gin_ref[0, at, :] = gr_ref[0, at, :]
            return
        z = product3(d_ref[0, at, :], wg3[...])
        to_res = scale_c * z[:, 0:base] + zi[:, 0:base]
        to_skip = scale_c * z[:, base:] + zi[:, base:]
        if kind == "some":
            m = mask_rows(start + n * rows + q, HALF, length)
            to_res, to_skip = to_res * m, to_skip * m
        res_ref[0, at, :] = (x + to_res) + br
        skip_ref[0, at, :] = to_skip + bs

    def lift(k):
        for s in blocks(width):
            for q in range(k * rows, (k + 1) * rows, SUB):
                at = slice(q, q + SUB)
                ext[2 * TAP + q : 2 * TAP + q + SUB, s] = (
                    c0[:, s] * f0_ref[0, at, s] - f1_ref[0, at, s] * (cc[:, s] + beta[:, s] * d_ref[0, at, s])
                )

    interleave(spread(0), [functools.partial(lift, k) for k in range(parts)])
    for n in range(parts):
        def step(kind, n=n):
            ahead = spread(n + 1) if n + 1 < parts else []
            shown = [functools.partial(outputs, n, kind, q) for q in range(0, rows, HALF)]
            if kind == "none":
                for piece in ahead + shown:
                    piece()
                return
            vector = elementwise(n, kind == "some")
            weights, *outs = products(n)
            each = len(vector) // len(outs)
            for j, out in enumerate(outs):
                interleave(ahead[j : j + 1] + shown[j : j + 1], vector[j * each : (j + 1) * each])
                out()
            weights()

        t0 = start + n * rows
        full, none = t0 + rows <= length, t0 >= length
        pl.when(full)(functools.partial(step, "full"))
        pl.when(jnp.logical_not(full | none))(functools.partial(step, "some"))
        pl.when(none)(functools.partial(step, "none"))

    @pl.when(i == items - 1)
    def _():
        outer = lax.dot_general(
            ch_ref[:, R_GM, 0 : 2 * base], coef[2], (((0,), (0,)), ((), ())),
            precision=lax.Precision.HIGHEST, preferred_element_type=f32,
        )
        both = (gwt[...] + outer).T
        done = acc[...].sum(axis=1)
        tap_sums = 2.0 * done[2:5]
        by_v = 0.5 * (tap0 * tap_sums[0:1] + tap1 * tap_sums[1:2] + tap2 * tap_sums[2:3])
        slope = (-2.0 / (1.0 - a1)) * (chan[1:2, :] + by_v - done[1:2])
        table = jnp.concatenate([done[0:1], slope, chan[2:4, :], chan[4:7, :] + tap_sums, chan[7:16, :]], axis=0)
        bias = bias_ref[...].sum(axis=0, keepdims=True)
        tail = jnp.concatenate([bias[:, 0:base], bias[:, base:], jnp.zeros((6, base), f32)], axis=0)
        pieces = [both[:, 0:base], both[:, base:]] + [gw[:, s] for s in blocks(width)]
        pieces += [table[:, s] for s in blocks(width)] + [tail]
        half = keep_ref.shape[0]
        pieces.append(jnp.zeros((2 * half - sum(p.shape[0] for p in pieces), LANES), f32))

        def store(first, second):
            at = 0
            for piece in pieces:
                end = at + piece.shape[0]
                for side, ref in enumerate((first, second)):
                    a, b = max(at, side * half), min(end, (side + 1) * half)
                    if a < b:
                        ref[a - side * half : b - side * half, :] = piece[a - at : b - at]
                at = end

        pl.when(mine_ref[0] == 0)(functools.partial(store, keep_ref, send_ref))
        pl.when(mine_ref[0] == 1)(functools.partial(store, send_ref, keep_ref))


def sum_rows(size):
    return -(-size // 256) * 256


def exchange(x, axis):
    return lax.all_to_all(x, axis, 0, 0)


def halves(n_item):
    return [1 << k for k in range(n_item.bit_length() - 1)]


def reduce_all(x, sizes, beside):
    n_tm, n_item = sizes["tm"], sizes["item"]
    keep, send = x

    def swap(y, by):
        return lax.ppermute(y, "item", [(d, d ^ by) for d in range(n_item)])

    for by in halves(n_item):
        if by > 1:
            half = x.shape[0] // 2
            mine = (lax.axis_index("item") // by) % 2
            keep = lax.dynamic_slice_in_dim(x, mine * half, half)
            send = lax.dynamic_slice_in_dim(x, (1 - mine) * half, half)
        x = keep + swap(send, by)
    if n_item == 1:
        x = jnp.concatenate([keep, send])
    parts = exchange(x.reshape((n_tm, x.shape[0] // n_tm) + x.shape[1:]), "tm")
    x = jnp.sum(parts, axis=0)
    x = exchange(jnp.broadcast_to(x[None], (n_tm,) + x.shape), "tm").reshape((-1,) + x.shape[1:])
    for by in halves(n_item)[::-1]:
        if by == 1:
            x, beside = lax.optimization_barrier((x, beside))
        mine = (lax.axis_index("item") // by) % 2
        other = swap(x, by)
        x = jnp.where(mine == 0, jnp.concatenate([x, other]), jnp.concatenate([other, x]))
    return x, beside


def whole(shape):
    return pl.BlockSpec(shape, lambda i: (0,) * len(shape))


def per_item(shape):
    return pl.BlockSpec((1,) + shape, lambda i: (i,) + (0,) * len(shape))


SMEM = pl.BlockSpec(memory_space=pltpu.SMEM)


def body(
    inputs, lengths, counts, weight_in, bias_in, slope_in, gain_in, shift_in, channelwise_taps, channelwise_bias,
    slope_out, gain_out, shift_out, weight_res, bias_res, weight_skip, bias_skip, grad_residual, grad_skip,
):
    items, frames, base = inputs.shape
    width = weight_in.shape[1]
    sources = grad_skip.shape[1]
    tm, across = lax.axis_size("tm"), lax.axis_size("item")
    place = lax.axis_index("tm").astype(jnp.int32).reshape(1)
    mine = (lax.axis_index("item") % 2).astype(jnp.int32).reshape(1)
    up = [(d, d + 1) for d in range(tm - 1)]
    down = [(d + 1, d) for d in range(tm - 1)]
    x_before = lax.ppermute(inputs[:, frames - TAP :], "tm", up)
    x_after = lax.ppermute(inputs[:, :TAP], "tm", down)

    def row(v):
        return v.reshape(1, -1)

    table = [row(bias_in), row(slope_in), row(gain_in), row(shift_in), channelwise_taps, row(channelwise_bias),
             row(slope_out), row(gain_out), row(shift_out)]
    table_specs = [whole(t.shape) for t in table]
    vmem = lambda mib: pltpu.CompilerParams(vmem_limit_bytes=mib * 2**20)

    rows1, rows2, rows3 = (min(c, frames) for c in (CHUNK1, CHUNK2, CHUNK3))
    v1, st1, ch1 = pl.pallas_call(
        functools.partial(first_kernel, rows1),
        grid=(items,),
        in_specs=[SMEM, SMEM, per_item((frames, base)),
                  pl.BlockSpec((1, rows1, base), lambda i: (jnp.minimum(i + 1, items - 1), 0, 0)),
                  whole((base, width)), whole((1, width)), whole((1, width))],
        out_specs=[per_item((frames, width)), whole((tm, items, LANES)), whole((items, 8, width))],
        out_shape=[jax.ShapeDtypeStruct((items, frames, width), f32), jax.ShapeDtypeStruct((tm, items, LANES), f32),
                   jax.ShapeDtypeStruct((items, 8, width), f32)],
        scratch_shapes=[pltpu.VMEM((3 * base, width), bf16), pltpu.VMEM((2, 8, width), f32)]
        + [pltpu.VMEM((rows1, width), f32)] * 2,
        compiler_params=vmem(58),
        name="first",
    )(lengths, place, inputs, inputs, weight_in, table[0], table[1])
    ga1 = exchange(st1, "tm")

    big = jax.ShapeDtypeStruct((items, frames, width), f32)
    f0, f1, d2, y, ch, st2, bias = pl.pallas_call(
        functools.partial(second_kernel, rows2),
        grid=(items,),
        in_specs=[SMEM, SMEM, SMEM, per_item((frames, width)), per_item((TAP, base)), per_item((TAP, base)),
                  per_item((frames, base)), per_item((sources, frames, base)), whole((base, width)),
                  whole((width, base)), whole((width, base))] + table_specs + [whole((tm, items, LANES))],
        out_specs=[per_item((frames, width))] * 3 + [per_item((2 * base, width)),
                   whole((items, ROWS, width)), whole((tm, items, LANES)), whole((8, 2 * base))],
        out_shape=[big, big, big, jax.ShapeDtypeStruct((items, 2 * base, width), f32), jax.ShapeDtypeStruct((items, ROWS, width), f32),
                   jax.ShapeDtypeStruct((tm, items, LANES), f32), jax.ShapeDtypeStruct((8, 2 * base), f32)],
        scratch_shapes=[pltpu.VMEM((3 * base, width), bf16), pltpu.VMEM((6 * base, width), bf16),
                        pltpu.VMEM((2, items, LANES), f32),
                        pltpu.VMEM((frames + 2 * TAP, width), f32), pltpu.VMEM((ROWS, 8, width), f32),
                        pltpu.VMEM((8, 2 * base), f32), pltpu.VMEM((2 * base, width), f32)]
        + [pltpu.VMEM((rows2, width), f32)] * 2 + [pltpu.VMEM((2, rows2, width), bf16)] * 2
        + [pltpu.VMEM((frames // rows2, 2, rows2, 2 * base), bf16)],
        compiler_params=vmem(48),
        name="second",
    )(lengths, counts, place, v1, x_before, x_after, grad_residual, grad_skip, weight_in, weight_res, weight_skip,
      *table, ga1)
    ga2 = exchange(st2, "tm")

    n_sum = sum_rows(2 * width + 4 * base + 64 + 8)
    out = jax.ShapeDtypeStruct((items, frames, base), f32)
    strip = lambda k: pl.BlockSpec((1, TAP, width), lambda i: (i, k, 0))
    last = frames // TAP - 1
    small = [((5, items, LANES), f32), ((3, items, width), f32), ((16, width), f32), ((items, 2 * base), f32),
             ((base, width), f32), ((8, 8, width), f32)]
    to_last, to_next, *given = pl.pallas_call(
        functools.partial(edge_kernel, frames),
        grid=(items,),
        in_specs=[SMEM, SMEM, per_item((TAP, base)), per_item((TAP, base))] + [strip(0), strip(last)] * 3
        + [whole((items, 8, width)), whole((items, ROWS, width)), whole((base, width)), whole((width, base)),
           whole((width, base))] + table_specs + [whole((tm, items, LANES))] * 2,
        out_specs=[per_item((TAP, base))] * 2 + [whole(shape) for shape, _ in small],
        out_shape=[jax.ShapeDtypeStruct((items, TAP, base), f32)] * 2
        + [jax.ShapeDtypeStruct(shape, dtype) for shape, dtype in small],
        scratch_shapes=[pltpu.VMEM((3 * base, width), bf16), pltpu.VMEM((3 * width, base), bf16)],
        compiler_params=vmem(48),
        name="edge",
    )(lengths, place, x_before, x_after, f0, f0, f1, f1, d2, d2, ch1, ch, weight_in, weight_res, weight_skip, *table,
      ga1, ga2)
    from_next = lax.ppermute(to_last, "tm", down)
    from_last = lax.ppermute(to_next, "tm", up)

    res, skip, gin, *sums = pl.pallas_call(
        functools.partial(third_kernel, rows3),
        grid=(items,),
        in_specs=[SMEM, SMEM, SMEM, per_item((frames, width)), per_item((frames, base)), per_item((frames, width)),
                  per_item((frames, width)), per_item((frames, width)), per_item((frames, base)),
                  per_item((2 * base, width)), whole((items, ROWS, width)),
                  whole((8, 2 * base)), whole((base, width)), whole((width, base)), whole((width, base)),
                  whole((1, base)), whole((1, base))]
        + [whole(shape) for shape, _ in small] + table_specs,
        out_specs=[per_item((frames, base))] * 3 + [whole((n_sum // 2, base))] * 2,
        out_shape=[out, out, out] + [jax.ShapeDtypeStruct((n_sum // 2, base), f32)] * 2,
        scratch_shapes=[pltpu.VMEM((3 * base, width), bf16), pltpu.VMEM((width, 2 * base), bf16),
                        pltpu.VMEM((3 * width, 2 * base), bf16),
                        pltpu.VMEM((frames + 4 * TAP, width), f32),
                        pltpu.VMEM((base, width), f32), pltpu.VMEM((2 * base, width), f32),
                        pltpu.VMEM((8, 8, width), f32)]
        + [pltpu.VMEM((rows3, width), f32)] * 2 + [pltpu.VMEM((2, rows3, width), bf16)] * 2,
        compiler_params=vmem(48),
        cost_estimate=pl.CostEstimate(flops=items * frames * width * base * 30, transcendentals=items * frames * width,
                                      bytes_accessed=items * frames * (5 * width + 7 * base) * 4),
        name="third",
    )(lengths, place, mine, v1, inputs, f0, f1, d2, grad_residual, y, ch, bias, weight_in, weight_res, weight_skip, row(bias_res), row(bias_skip),
      *given, *table)

    sums, from_next, from_last = lax.optimization_barrier((sums, from_next, from_last))
    gin = gin.at[:, frames - TAP :].add(from_next)
    gin = gin.at[:, :TAP].add(from_last)
    total, gin = reduce_all(sums, {"tm": tm, "item": across}, gin)

    g_res, g_skip = total[0:width], total[width : 2 * width]
    at0 = 2 * width + 4 * base
    g_in = total[2 * width : at0].reshape(4, base, LANES).transpose(1, 0, 2).reshape(base, width)
    vec = total[at0 : at0 + 64].reshape(4, 16, LANES).transpose(1, 0, 2).reshape(16, width)
    return (
        res, skip, gin, g_in, vec[0], vec[1], vec[2], vec[3], vec[4:7], vec[7], vec[8], vec[9], vec[10],
        g_res, total[at0 + 64], g_skip, total[at0 + 65],
    )


def solution(mesh):
    spread = P("item", "tm", None)
    return jax.shard_map(
        body,
        mesh=mesh,
        in_specs=(spread, P("item"), P("item")) + (P(),) * 14 + (spread, P("item", None, "tm", None)),
        out_specs=(spread,) * 3 + (P(),) * 14,
        check_vma=False,
    )
```

```python
import functools

import jax
import jax.numpy as jnp
from jax import lax
from jax.experimental import pallas as pl
from jax.experimental.pallas import tpu as pltpu
from jax.sharding import PartitionSpec as P

TAP = 128
LANES = 128
EPSILON = 1e-05
LN2 = 0.6931471805599453
f32 = jnp.float32
bf16 = jnp.bfloat16

PARAMS = ("bias_in", "slope_in", "gain_in", "shift_in", "taps", "bias_dw", "slope_out", "gain_out", "shift_out")
(R_P, R_S, R_SS, R_GD, R_GS, R_H0, R_H1, R_H2, R_HF0, R_HF1, R_HF2, R_PF0, R_PF1, R_PF2,
 R_A0, R_A1, R_A2, R_Z0, R_Z1, R_Z2, R_GM) = range(21)
ROWS = 24
SUB = 32
HALF = 128
CHUNK1, CHUNK2, CHUNK3 = 512, 256, 256


def split(x):
    hi = x.astype(bf16)
    lo = (x - hi.astype(f32)).astype(bf16)
    return hi, lo


def dot(a, b):
    return jnp.dot(a, b, preferred_element_type=f32)


def dot0(a, b):
    return lax.dot_general(a, b, (((0,), (0,)), ((), ())), preferred_element_type=f32)


def product3(x, w3):
    hi, lo = split(x)
    return dot(jnp.concatenate([hi, hi, lo], axis=1), w3)


def stacked3(w):
    hi, lo = split(w)
    return jnp.concatenate([hi, lo, hi], axis=0)


def half_act(h, a, c):
    t = jnp.tanh(h)
    return jnp.maximum(h, a * h) - c * jnp.log2(1.0 + jnp.abs(t)), t


def fold(x):
    rows, cols = x.shape
    return x.reshape(rows // 8, 8, cols).sum(axis=0)


def mask_rows(first, rows, length):
    row = lax.broadcasted_iota(jnp.int32, (rows, 1), 0) + first
    return ((row >= 0) & (row < length)).astype(f32)


def lane_put(values):
    shape = values[0].shape[:-1] + (LANES,)
    lane = lax.broadcasted_iota(jnp.int32, shape, len(shape) - 1)
    out = jnp.zeros(shape, f32)
    for k, v in enumerate(values):
        out = jnp.where(lane == k, jnp.broadcast_to(v, shape), out)
    return out


def channel(ref):
    def get(name):
        if name.startswith("tap"):
            k = int(name[3])
            return ref["taps"][k : k + 1]
        return ref[name][...]

    return get


def interleave(first, second):
    done = 0
    for n, piece in enumerate(first):
        piece()
        upto = (n + 1) * len(second) // len(first)
        for other in second[done:upto]:
            other()
        done = upto
    for other in second[done:]:
        other()


def blocks(width):
    return [slice(j * LANES, (j + 1) * LANES) for j in range(width // LANES)]


def per_item_column(values):
    row = lax.broadcasted_iota(jnp.int32, (len(values), 1), 0)
    out = jnp.zeros((len(values), 1), f32)
    for k, v in enumerate(values):
        out = jnp.where(row == k, v, out)
    return out


def frames_here(len_ref, start, frames, items):
    return per_item_column([jnp.clip(len_ref[k] - start, 0, frames).astype(f32) for k in range(items)])


def first_kernel(rows, len_ref, tm_ref, x_ref, xn_ref, w_ref, b_ref, a_ref, v_ref, st_ref, ch_ref, w3, acc, hb0, hb1):
    i = pl.program_id(0)
    items = ch_ref.shape[0]
    frames, width = v_ref.shape[1:]
    slots = (hb0, hb1)

    @pl.when(i == 0)
    def _():
        w3[...] = stacked3(0.5 * w_ref[...])
        hb0[...] = product3(x_ref[0, 0:rows, :], w3[...])

    length = len_ref[i]
    start = tm_ref[0] * frames
    b, a = 0.5 * b_ref[...], a_ref[...]
    c = (1.0 - a) * (0.5 * LN2)
    centre = half_act(hb0[0:8, :] + b, a, c)[0][0:1]
    parts = frames // rows

    for k in range(parts):
        def step(masked, k=k):
            h, then = slots[k % 2], slots[(k + 1) % 2]
            if masked:
                m = mask_rows(start + k * rows, rows, length)

            def ahead(q):
                x = x_ref[0, (k + 1) * rows + q : (k + 1) * rows + q + HALF, :] if k < parts - 1 else xn_ref[0, q : q + HALF, :]
                then[q : q + HALF, :] = product3(x, w3[...])

            def unit(s):
                total = square = jnp.zeros((8, LANES), f32)
                for q in range(0, rows, SUB):
                    v, _ = half_act(h[q : q + SUB, s] + b[:, s], a[:, s], c[:, s])
                    v_ref[0, k * rows + q : k * rows + q + SUB, s] = v
                    d = v - centre[:, s]
                    dm = d * m[q : q + SUB] if masked else d
                    total = total + fold(dm)
                    square = square + fold(dm * d)
                acc[0, :, s] = total if k == 0 else acc[0, :, s] + total
                acc[1, :, s] = square if k == 0 else acc[1, :, s] + square

            interleave([functools.partial(ahead, q) for q in range(0, rows, HALF)],
                       [functools.partial(unit, s) for s in blocks(width)])

        full = start + (k + 1) * rows <= length
        pl.when(full)(functools.partial(step, False))
        pl.when(jnp.logical_not(full))(functools.partial(step, True))

    ch_ref[pl.ds(i, 1), 0, :] = acc[0].sum(axis=0, keepdims=True)
    ch_ref[pl.ds(i, 1), 1, :] = acc[1].sum(axis=0, keepdims=True)
    ch_ref[pl.ds(i, 1), 2, :] = centre

    @pl.when(i == items - 1)
    def _():
        n = frames_here(len_ref, start, frames, items)
        safe = jnp.maximum(n, 1.0)
        total, square, centre = ch_ref[:, 0, :], ch_ref[:, 1, :], ch_ref[:, 2, :]
        ch_ref[:, 0, :] = total + n * centre
        ch_ref[:, 1, :] = square + 2.0 * centre * total + n * centre * centre
        total = total / safe
        level = centre + c + total
        mean = level.sum(axis=1, keepdims=True) / width
        dev = level - mean
        spread = (square - safe * total * total + safe * dev * dev).sum(axis=1, keepdims=True)
        some = (n > 0).astype(f32)
        st_ref[...] = jnp.broadcast_to(lane_put([2.0 * mean * some, 4.0 * spread * some, n])[None], st_ref.shape)


def merged(gathered, width):
    mean_d, spread_d, n_d = gathered[:, :, 0:1], gathered[:, :, 1:2], gathered[:, :, 2:3]
    n = n_d.sum(axis=0)
    mean = (n_d * mean_d).sum(axis=0) / n
    dev = mean_d - mean[None]
    spread = (spread_d + n_d * width * dev * dev).sum(axis=0)
    count = n * width
    return mean, lax.rsqrt(spread / count + EPSILON), count


def wide(x, width):
    return jnp.broadcast_to(x[:, 0:1], (x.shape[0], width))


def second_kernel(
    rows, len_ref, cnt_ref, tm_ref, v_ref, xb_ref, xa_ref, gr_ref, gk_ref, w_ref, wr_ref, ws_ref, *rest
):
    params, rest = rest[: len(PARAMS)], rest[len(PARAMS) :]
    ga_ref, f0_ref, f1_ref, d_ref, y_ref, ch_ref, st_ref, bias_ref, *rest = rest
    w3, wt3, stat, fst, acc, gacc, yacc, gs0, gs1, hl0, hl1, gb = rest
    par = channel(dict(zip(PARAMS, params)))
    i = pl.program_id(0)
    items = ch_ref.shape[0]
    frames, width = v_ref.shape[1:]
    base = gr_ref.shape[2]
    parts = frames // rows
    gs_slots, hl_slots = (gs0, gs1), (hl0, hl1)

    @pl.when(i == 0)
    def _():
        w3[...] = stacked3(0.5 * w_ref[...])
        both = jnp.concatenate([wr_ref[...], ws_ref[...]], axis=1)
        wt3[...] = stacked3(both.T)
        mean, scale, _ = merged(ga_ref[...], width)
        stat[0] = jnp.broadcast_to(mean, stat.shape[1:])
        stat[1] = jnp.broadcast_to(scale, stat.shape[1:])
        bias_ref[...] = jnp.zeros_like(bias_ref)
        ch_ref[...] = jnp.zeros_like(ch_ref)

    length = len_ref[i]
    start = tm_ref[0] * frames
    mean = wide(stat[0, pl.ds(i, 1), :], width)
    scale = wide(stat[1, pl.ds(i, 1), :], width)
    a1 = par("slope_in")
    c1 = (1.0 - a1) * (0.5 * LN2)
    gain = 2.0 * par("gain_in") * scale
    shift = par("shift_in") + gain * (c1 - 0.5 * mean)
    b1 = 0.5 * par("bias_in")
    alive = [(s < cnt_ref[i]).astype(f32) for s in range(gk_ref.shape[1])]
    taps = [0.5 * par(f"tap{k}") for k in range(3)]
    bias = 0.5 * par("bias_dw")
    a2 = par("slope_out")
    c2 = (1.0 - a2) * (0.5 * LN2)
    d_base, d_gain = 0.5 + 0.5 * a2, 0.5 - 0.5 * a2

    def cotangents(k):
        at = slice(k * rows, (k + 1) * rows)
        g_res = gr_ref[0, at, :]
        g_skip = alive[0] * gk_ref[0, 0, at, :]
        for s in range(1, len(alive)):
            g_skip = g_skip + alive[s] * gk_ref[0, s, at, :]
        return jnp.concatenate([g_res, g_skip], axis=1)

    def spread(k):
        def prepare():
            both = cotangents(k)
            bias_ref[...] += fold(both)
            row = lax.broadcasted_iota(jnp.int32, (rows, 1), 0)
            both = jnp.where(row < length - start - k * rows, both, 0.0)
            gacc[...] = fold(both) if k == 0 else gacc[...] + fold(both)
            ghi, glo = split(both)
            gb[k, 0], gb[k, 1] = ghi, glo

        def multiply(q):
            if q == 0:
                prepare()
            ghi, glo = gb[k, 0, q : q + HALF, :], gb[k, 1, q : q + HALF, :]
            gs_slots[k % 2][q : q + HALF, :] = dot(jnp.concatenate([ghi, ghi, glo], axis=1), wt3[...])

        return [functools.partial(multiply, q) for q in range(0, rows, HALF)]

    def products(k):
        hl = hl_slots[k % 2]

        def weights(q):
            at = slice(q, q + base)
            ghi, glo = gb[k, 0, :, at], gb[k, 1, :, at]
            y = dot0(jnp.concatenate([ghi, ghi, glo], axis=0), jnp.concatenate([hl[0], hl[1], hl[0]], axis=0))
            if k == parts - 1:
                y_ref[0, at, :] = yacc[at, :] + y if k else y
            else:
                yacc[at, :] = yacc[at, :] + y if k else y

        return [functools.partial(weights, q) for q in (0, base)]

    h = product3(jnp.concatenate([xb_ref[0], xa_ref[0]], axis=0), w3[...])
    for piece in spread(0):
        piece()
    for side, at in ((0, 0), (1, frames + TAP)):
        m = mask_rows(start + at - TAP, TAP, length)
        for s in blocks(width):
            for q in range(0, TAP, SUB):
                v, _ = half_act(h[side * TAP + q : side * TAP + q + SUB, s] + b1[:, s], a1[:, s], c1[:, s])
                fst[at + q : at + q + SUB, s] = m[q : q + SUB] * (gain[:, s] * v + shift[:, s])

    def lift(k, _):
        r0 = pl.multiple_of(k * TAP, TAP)
        full = start + r0 + TAP <= length

        @pl.when(full)
        def _():
            fst[pl.ds(TAP + r0, TAP), :] = gain * v_ref[0, pl.ds(r0, TAP), :] + shift

        @pl.when(jnp.logical_not(full))
        def _():
            m = mask_rows(start + r0, TAP, length)
            fst[pl.ds(TAP + r0, TAP), :] = m * (gain * v_ref[0, pl.ds(r0, TAP), :] + shift)

        return 0

    lax.fori_loop(0, frames // TAP, lift, 0)

    def halved(r, size, s):
        return (
            taps[0][:, s] * fst[r : r + size, s]
            + taps[1][:, s] * fst[r + TAP : r + TAP + size, s]
            + taps[2][:, s] * fst[r + 2 * TAP : r + 2 * TAP + size, s]
            + bias[:, s]
        )

    point = jnp.concatenate(
        [half_act(halved(0, 8, s), a2[:, s], c2[:, s])[0][0:1] for s in blocks(width)], axis=1
    )
    tracked = [r for r in range(R_S, R_A0) if r != R_GS]

    def elementwise(k, masked):
        gs, hl = gs_slots[k % 2], hl_slots[k % 2]
        if masked:
            m = mask_rows(start + k * rows, rows, length)

        def unit(s, begin):
            zero = jnp.zeros((8, LANES), f32)
            sums = {r: zero for r in tracked}
            for q in range(begin, begin + HALF, SUB):
                at = slice(k * rows + q, k * rows + q + SUB)
                f = halved(k * rows + q, SUB, s)
                v, t = half_act(f, a2[:, s], c2[:, s])
                dm = d_base[:, s] + d_gain[:, s] * t
                d = v - point[:, s]
                g = gs[q : q + SUB, s]
                dd, fm = d, f
                if masked:
                    mq = m[q : q + SUB]
                    dm, dd, fm = dm * mq, d * mq, f * mq
                f0 = g * dm
                f2 = d * dm
                f0_ref[0, at, s] = f0
                f1_ref[0, at, s] = dm
                d_ref[0, at, s] = d
                for r, x in (
                    (R_S, dd), (R_SS, dd * d), (R_GD, g * d), (R_H0, f0), (R_H1, dm), (R_H2, f2), (R_HF0, f0 * f),
                    (R_HF1, dm * f), (R_HF2, f2 * f), (R_PF0, g * f), (R_PF1, fm), (R_PF2, dd * f),
                ):
                    sums[r] = sums[r] + fold(x)
                hi, lo = split(d)
                hl[0, q : q + SUB, s] = hi
                hl[1, q : q + SUB, s] = lo
            for r, x in sums.items():
                acc[r, :, s] = x if k == 0 and begin == 0 else acc[r, :, s] + x

        return [functools.partial(unit, s, q) for q in range(0, rows, HALF) for s in blocks(width)]

    def nothing(k):
        at = slice(k * rows, (k + 1) * rows)
        zero = jnp.zeros((rows, width), f32)
        for ref in (f0_ref, f1_ref, d_ref):
            ref[0, at, :] = zero
        hl_slots[k % 2][...] = jnp.zeros_like(hl0)
        if k == 0:
            for r in tracked:
                acc[r] = jnp.zeros((8, width), f32)

    for k in range(parts):
        def step(kind, k=k):
            matrix = (spread(k + 1) if k + 1 < parts else []) + (products(k - 1) if k > 0 else [])
            interleave(matrix, [functools.partial(nothing, k)] if kind == "none" else elementwise(k, kind == "some"))

        t0 = start + k * rows
        full, none = t0 + rows <= length, t0 >= length
        pl.when(full)(functools.partial(step, "full"))
        pl.when(jnp.logical_not(full | none))(functools.partial(step, "some"))
        pl.when(none)(functools.partial(step, "none"))
    for piece in products(parts - 1):
        piece()

    edges = acc.at[pl.ds(R_A0, 6)]
    edges[...] = jnp.zeros(edges.shape, f32)

    def edge(k, _):
        r0 = pl.multiple_of(k * TAP, TAP)
        t0 = start + r0
        for row, near in ((R_A0, t0 < TAP), (R_Z0, (t0 < length) & (t0 + TAP > length - TAP))):
            @pl.when(near)
            def _():
                at = lax.broadcasted_iota(jnp.int32, (TAP, 1), 0) + t0
                there = ((at < TAP) if row == R_A0 else (at >= length - TAP)).astype(f32)
                f1 = there * f1_ref[0, pl.ds(r0, TAP), :]
                acc[row] += fold(there * f0_ref[0, pl.ds(r0, TAP), :])
                acc[row + 1] += fold(f1)
                acc[row + 2] += fold(f1 * d_ref[0, pl.ds(r0, TAP), :])
        return 0

    lax.fori_loop(0, frames // TAP, edge, 0)

    ch_ref[pl.ds(i, 1), R_GM, 0 : 2 * base] = gacc[...].sum(axis=0, keepdims=True)
    ch_ref[pl.ds(i, 1), R_P, :] = 2.0 * (point + c2)
    for r in range(R_S, R_GM):
        if r != R_GS:
            total = acc[r].sum(axis=0, keepdims=True)
            if r in (R_S, R_GD, R_H2, R_HF0, R_HF1, R_PF0, R_PF1, R_A2, R_Z2):
                total = 2.0 * total
            if r in (R_SS, R_HF2, R_PF2):
                total = 4.0 * total
            ch_ref[pl.ds(i, 1), r, :] = total

    @pl.when(i == items - 1)
    def _():
        gm = jnp.concatenate([ch_ref[:, R_GM, 0 : 2 * base]] * 2, axis=0)
        ch_ref[:, R_GS, :] = product3(gm, wt3[...])[0:items]

        def got(r):
            return ch_ref[:, r, :]

        n = frames_here(len_ref, start, frames, items)
        some = (n > 0).astype(f32)
        safe = jnp.maximum(n, 1.0)
        point, offset = got(R_P), got(R_S) / safe
        level = point + offset
        mean2 = level.sum(axis=1, keepdims=True) / width
        dev = level - mean2
        spread2 = (got(R_SS) - safe * offset * offset + safe * dev * dev).sum(axis=1, keepdims=True)
        point = point - mean2
        gout = par("gain_out")
        tap0, tap1, tap2 = par("tap0"), par("tap1"), par("tap2")
        g1, sh1, cb = par("gain_in"), par("shift_in"), par("bias_dw")

        def summed(x):
            return x.sum(axis=1, keepdims=True)

        s1 = summed(gout * got(R_GS))
        s2 = summed(gout * (got(R_GD) + point * got(R_GS)))
        t1, t2 = [], []
        for q in range(3):
            h, hf, h_a, h_z = got(R_H0 + q), got(R_HF0 + q), got(R_A0 + q), got(R_Z0 + q)
            if q == 0:
                h, hf, h_a, h_z = gout * h, gout * hf, gout * h_a, gout * h_z
            if q == 2:
                h, hf = h + point * got(R_H1), hf + point * got(R_HF1)
                h_a, h_z = h_a + point * got(R_A1), h_z + point * got(R_Z1)
            kh = (tap0 + tap1 + tap2) * h - tap0 * h_a - tap2 * h_z
            t1.append(summed(g1 * kh))
            t2.append(summed(hf - cb * h - sh1 * kh))
        row = lane_put([mean2 * some, spread2 * some, n, s1, s2] + t1 + t2)
        st_ref[...] = jnp.broadcast_to(row[None], st_ref.shape)


def edge_kernel(
    frames, len_ref, tm_ref, xb_ref, xa_ref, f0a_ref, f0z_ref, f1a_ref, f1z_ref, da_ref, dz_ref,
    ch1_ref, ch_ref, w_ref, wr_ref, ws_ref, *rest
):
    params, rest = rest[: len(PARAMS)], rest[len(PARAMS) :]
    ga1_ref, ga2_ref, before_ref, after_ref, stat_ref, coef_ref, chan_ref, zc_ref, gw, acc, w3, wt3 = rest
    par = channel(dict(zip(PARAMS, params)))
    i = pl.program_id(0)
    width = f0a_ref.shape[2]
    tap0, tap1, tap2 = par("tap0"), par("tap1"), par("tap2")
    a1 = par("slope_in")
    c1 = (1.0 - a1) * (0.5 * LN2)

    def put(k, x):
        stat_ref[k] = jnp.broadcast_to(x, stat_ref.shape[1:])

    @pl.when(i == 0)
    def _():
        w3[...] = stacked3(0.5 * w_ref[...])
        wt3[...] = stacked3(w_ref[...].T)
        mean1, scale1, count = merged(ga1_ref[...], width)
        mean2, scale2, _ = merged(ga2_ref[...], width)
        g = ga2_ref[...]

        def lane(k):
            return g[:, :, k : k + 1]

        dev = lane(0) - mean2[None]
        s1 = lane(3).sum(axis=0)
        s2 = (lane(4) + dev * lane(3)).sum(axis=0)
        alpha = scale2 * s1 / count
        beta = scale2 * scale2 * scale2 * s2 / count
        t1 = scale2 * lane(5).sum(axis=0) - alpha * lane(6).sum(axis=0) - beta * (lane(7) + dev * lane(6)).sum(axis=0)
        t2 = scale2 * lane(8).sum(axis=0) - alpha * lane(9).sum(axis=0) - beta * (lane(10) + dev * lane(9)).sum(axis=0)
        cut = scale1 * t1 / count
        cut_v = scale1 * scale1 * t2 / count
        put(0, scale1)
        put(1, scale2)
        put(2, 2.0 * beta)
        put(3, cut - cut_v * mean1)
        put(4, 2.0 * cut_v)
        delta = ch_ref[:, R_P, :] - mean2
        coef_ref[0] = scale2 * par("gain_out")
        coef_ref[1] = alpha + beta * delta
        coef_ref[2] = scale2 * par("gain_out") * delta + par("shift_out")
        both = jnp.concatenate([wr_ref[...], ws_ref[...]], axis=1)
        zc_ref[...] = lax.dot_general(
            coef_ref[2], both, (((1,), (0,)), ((), ())), precision=lax.Precision.HIGHEST, preferred_element_type=f32
        )

        def row(r):
            return ch_ref[:, r, :]

        c0, cc = coef_ref[0], coef_ref[1]

        def comb(r):
            return c0 * row(r) - cc * row(r + 1) - beta * row(r + 2)

        h, hf, h_a, h_z = comb(R_H0), comb(R_HF0), comb(R_A0), comb(R_Z0)
        kh = (tap0 + tap1 + tap2) * h - tap0 * h_a - tap2 * h_z
        n = ga2_ref[pl.ds(tm_ref[0], 1), :, 2:3][0]
        total = c0 * row(R_GS) - cc * n - beta * row(R_S)
        total_d = c0 * row(R_GD) - cc * row(R_S) - beta * row(R_SS)
        total_f = c0 * row(R_PF0) - cc * row(R_PF1) - beta * row(R_PF2)
        slope = (total_d + row(R_P) * total - total_f) / (1.0 - par("slope_out"))

        def over(x):
            return x.sum(axis=0, keepdims=True)

        gain_out = over(scale2 * row(R_GD) + (scale2 * delta) * row(R_GS))
        gain_in = over(hf - par("bias_dw") * h - par("shift_in") * kh) / par("gain_in")
        gain1 = par("gain_in") * scale1
        shift = par("shift_in") + gain1 * (2.0 * c1 - mean1)
        m1, m2 = ch1_ref[:, 0, :], ch1_ref[:, 1, :]
        k0 = cut - cut_v * mean1 + 2.0 * cut_v * c1
        k1 = 2.0 * cut_v
        act_sum = gain1 * kh - k0 * n - k1 * m1
        act_v = -(k0 * m1 + k1 * m2)
        zero = jnp.zeros((1, width), f32)
        chan_ref[...] = jnp.concatenate(
            [zero, over(c1 * act_sum + act_v), gain_in, over(kh), over(shift * (h - h_a)), over(shift * h),
             over(shift * (h - h_z)), over(h), -over(slope), gain_out, over(row(R_GS)), jnp.zeros((5, width), f32)],
            axis=0,
        )
        gw[...] = jnp.zeros_like(gw)
        acc[...] = jnp.zeros_like(acc)

    length = len_ref[i]
    start = tm_ref[0] * frames

    def st(k):
        return wide(stat_ref[k, pl.ds(i, 1), :], width)

    gain1, beta = par("gain_in") * st(0), st(2)
    c0, cc = coef_ref[0, pl.ds(i, 1), :], coef_ref[1, pl.ds(i, 1), :]
    b1 = 0.5 * par("bias_in")
    d_base, d_gain = 0.5 + 0.5 * a1, 0.5 - 0.5 * a1
    x = jnp.concatenate([xb_ref[0], xa_ref[0]], axis=0)
    xhi, xlo = split(x)
    h = dot(jnp.concatenate([xhi, xhi, xlo], axis=1), w3[...])
    masks = (mask_rows(start - TAP, TAP, length), mask_rows(start + frames, TAP, length))
    taps = (gain1 * tap0, gain1 * tap2)
    grads = ((f0a_ref, f1a_ref, da_ref), (f0z_ref, f1z_ref, dz_ref))
    his, los = [], []
    for side in range(2):
        f0, f1, d = grads[side]
        m = masks[side]
        hi_s, lo_s = [], []
        for s in blocks(width):
            sums = [jnp.zeros((8, LANES), f32)] * 3
            hi_q, lo_q = [], []
            for q in range(0, TAP, SUB):
                at = slice(q, q + SUB)
                hq = h[side * TAP + q : side * TAP + q + SUB, s] + b1[:, s]
                v, t = half_act(hq, a1[:, s], c1[:, s])
                grad = m[at] * (c0[:, s] * f0[0, at, s] - f1[0, at, s] * (cc[:, s] + beta[:, s] * d[0, at, s]))
                u = taps[side][:, s] * grad
                gh = u * (d_base[:, s] + d_gain[:, s] * t)
                for k, x_ in enumerate((gh, u * hq, grad * v)):
                    sums[k] = sums[k] + fold(x_)
                hi, lo = split(gh)
                hi_q.append(hi)
                lo_q.append(lo)
            acc[0, :, s] += sums[0]
            acc[1, :, s] += sums[1]
            acc[2 + 2 * side, :, s] += gain1[:, s] * sums[2]
            hi_s.append(jnp.concatenate(hi_q, axis=0))
            lo_s.append(jnp.concatenate(lo_q, axis=0))
        his.append(jnp.concatenate(hi_s, axis=1))
        los.append(jnp.concatenate(lo_s, axis=1))
    hi, lo = jnp.concatenate(his, axis=0), jnp.concatenate(los, axis=0)
    gw[...] += dot0(jnp.concatenate([xhi, xhi, xlo], axis=0), jnp.concatenate([hi, lo, hi], axis=0))
    back = dot(jnp.concatenate([hi, hi, lo], axis=1), wt3[...])
    before_ref[0], after_ref[0] = back[0:TAP], back[TAP:]


def third_kernel(
    rows, len_ref, tm_ref, mine_ref, v_ref, x_ref, f0_ref, f1_ref, d_ref, gr_ref, y_ref,
    ch_ref, bias_ref, w_ref, wr_ref, ws_ref, br_ref, bs_ref, stat, coef, chan, zc, gw0_ref, acc0_ref, *rest
):
    params, rest = rest[: len(PARAMS)], rest[len(PARAMS) :]
    res_ref, skip_ref, gin_ref, keep_ref, send_ref, *rest = rest
    w3, wt, wg3, ext, gw, gwt, acc, hb0, hb1, hl0, hl1 = rest
    par = channel(dict(zip(PARAMS, params)))
    i = pl.program_id(0)
    items = ch_ref.shape[0]
    frames, width = v_ref.shape[1:]
    base = gr_ref.shape[2]
    tap0, tap1, tap2 = par("tap0"), par("tap1"), par("tap2")
    a1 = par("slope_in")
    c1 = (1.0 - a1) * (0.5 * LN2)

    @pl.when(i == 0)
    def _():
        w3[...] = stacked3(0.5 * w_ref[...])
        wt[...] = jnp.concatenate(split(w_ref[...].T), axis=1)
        both = jnp.concatenate([wr_ref[...], ws_ref[...]], axis=1)
        wg3[...] = stacked3((both.T * (2.0 * par("gain_out"))).T)
        zeros = jnp.zeros((2 * TAP, width), f32)
        ext[0 : 2 * TAP, :] = zeros
        ext[frames + 2 * TAP : frames + 4 * TAP, :] = zeros
        gw[...] = gw0_ref[...]
        gwt[...] = jnp.zeros_like(gwt)
        acc[...] = acc0_ref[...]

    length = len_ref[i]
    start = tm_ref[0] * frames

    def st(k):
        return wide(stat[k, pl.ds(i, 1), :], width)

    scale1, scale2, beta, cut, cut_v = [st(k) for k in range(5)]
    c0, cc = coef[0, pl.ds(i, 1), :], coef[1, pl.ds(i, 1), :]
    gwt[...] += (2.0 * c0) * y_ref[0]
    gain1 = par("gain_in") * scale1
    cut = cut + cut_v * c1
    taps = [gain1 * tap0, gain1 * tap1, gain1 * tap2]
    b1 = 0.5 * par("bias_in")
    d_base, d_gain = 0.5 + 0.5 * a1, 0.5 - 0.5 * a1

    parts = frames // rows
    h_slots, hl_slots = (hb0, hb1), (hl0, hl1)

    def spread(n):
        def multiply(q):
            h_slots[n % 2][q : q + HALF, :] = product3(x_ref[0, n * rows + q : n * rows + q + HALF, :], w3[...])

        return [functools.partial(multiply, q) for q in range(0, rows, HALF)]

    def elementwise(n, masked):
        hb, hl = h_slots[n % 2], hl_slots[n % 2]
        if masked:
            m = mask_rows(start + n * rows, rows, length)

        def unit(s, begin):
            sums = [jnp.zeros((8, LANES), f32)] * 5
            for q in range(begin, begin + HALF, SUB):
                hq = hb[q : q + SUB, s] + b1[:, s]
                r = n * rows + q
                t = jnp.tanh(hq)
                v = v_ref[0, r : r + SUB, s]
                later = ext[r + 3 * TAP : r + 3 * TAP + SUB, s]
                here = ext[r + 2 * TAP : r + 2 * TAP + SUB, s]
                before = ext[r + TAP : r + TAP + SUB, s]
                u = taps[0][:, s] * later + taps[1][:, s] * here + taps[2][:, s] * before
                u = u - cut[:, s] - cut_v[:, s] * v
                vm = v
                if masked:
                    u, vm = u * m[q : q + SUB], v * m[q : q + SUB]
                gh = u * (d_base[:, s] + d_gain[:, s] * t)
                for k, x_ in enumerate((gh, u * hq, later * vm, here * vm, before * vm)):
                    sums[k] = sums[k] + fold(x_)
                hi, lo = split(gh)
                hl[0, q : q + SUB, s] = hi
                hl[1, q : q + SUB, s] = lo
            for k, x_ in enumerate(sums):
                acc[k, :, s] += x_ if k < 2 else gain1[:, s] * x_

        return [functools.partial(unit, s, q) for q in range(0, rows, HALF) for s in blocks(width)]

    def products(n):
        hl = hl_slots[n % 2]

        def weights():
            xhi, xlo = split(x_ref[0, n * rows : (n + 1) * rows, :])
            gw[...] += dot0(jnp.concatenate([xhi, xhi, xlo], axis=0), jnp.concatenate([hl[0], hl[1], hl[0]], axis=0))

        def out(q):
            hi, lo = hl[0, q : q + HALF, :], hl[1, q : q + HALF, :]
            at = slice(n * rows + q, n * rows + q + HALF)
            by_hi = dot(hi, wt[...])
            by_lo = dot(lo, wt[:, 0:base])
            gin_ref[0, at, :] = gr_ref[0, at, :] + (by_hi[:, 0:base] + (by_hi[:, base:] + by_lo))

        return [weights] + [functools.partial(out, q) for q in range(0, rows, HALF)]

    scale_c = stat[1, pl.ds(i, 1), :]
    br, bs = br_ref[...], bs_ref[...]
    zi = zc[pl.ds(i, 1), :]

    def outputs(n, kind, q):
        at = slice(n * rows + q, n * rows + q + HALF)
        x = x_ref[0, at, :]
        if kind == "none":
            res_ref[0, at, :] = x + br
            skip_ref[0, at, :] = jnp.broadcast_to(bs, (HALF, base))
            gin_ref[0, at, :] = gr_ref[0, at, :]
            return
        z = product3(d_ref[0, at, :], wg3[...])
        to_res = scale_c * z[:, 0:base] + zi[:, 0:base]
        to_skip = scale_c * z[:, base:] + zi[:, base:]
        if kind == "some":
            m = mask_rows(start + n * rows + q, HALF, length)
            to_res, to_skip = to_res * m, to_skip * m
        res_ref[0, at, :] = (x + to_res) + br
        skip_ref[0, at, :] = to_skip + bs

    def lift(k):
        for s in blocks(width):
            for q in range(k * rows, (k + 1) * rows, SUB):
                at = slice(q, q + SUB)
                ext[2 * TAP + q : 2 * TAP + q + SUB, s] = (
                    c0[:, s] * f0_ref[0, at, s] - f1_ref[0, at, s] * (cc[:, s] + beta[:, s] * d_ref[0, at, s])
                )

    interleave(spread(0), [functools.partial(lift, k) for k in range(parts)])
    for n in range(parts):
        def step(kind, n=n):
            ahead = spread(n + 1) if n + 1 < parts else []
            shown = [functools.partial(outputs, n, kind, q) for q in range(0, rows, HALF)]
            if kind == "none":
                for piece in ahead + shown:
                    piece()
                return
            vector = elementwise(n, kind == "some")
            weights, *outs = products(n)
            each = len(vector) // len(outs)
            for j, out in enumerate(outs):
                interleave(ahead[j : j + 1] + shown[j : j + 1], vector[j * each : (j + 1) * each])
                out()
            weights()

        t0 = start + n * rows
        full, none = t0 + rows <= length, t0 >= length
        pl.when(full)(functools.partial(step, "full"))
        pl.when(jnp.logical_not(full | none))(functools.partial(step, "some"))
        pl.when(none)(functools.partial(step, "none"))

    @pl.when(i == items - 1)
    def _():
        outer = lax.dot_general(
            ch_ref[:, R_GM, 0 : 2 * base], coef[2], (((0,), (0,)), ((), ())),
            precision=lax.Precision.HIGHEST, preferred_element_type=f32,
        )
        both = (gwt[...] + outer).T
        done = acc[...].sum(axis=1)
        tap_sums = 2.0 * done[2:5]
        by_v = 0.5 * (tap0 * tap_sums[0:1] + tap1 * tap_sums[1:2] + tap2 * tap_sums[2:3])
        slope = (-2.0 / (1.0 - a1)) * (chan[1:2, :] + by_v - done[1:2])
        table = jnp.concatenate([done[0:1], slope, chan[2:4, :], chan[4:7, :] + tap_sums, chan[7:16, :]], axis=0)
        bias = bias_ref[...].sum(axis=0, keepdims=True)
        tail = jnp.concatenate([bias[:, 0:base], bias[:, base:], jnp.zeros((6, base), f32)], axis=0)
        pieces = [both[:, 0:base], both[:, base:]] + [gw[:, s] for s in blocks(width)]
        pieces += [table[:, s] for s in blocks(width)] + [tail]
        half = keep_ref.shape[0]
        pieces.append(jnp.zeros((2 * half - sum(p.shape[0] for p in pieces), LANES), f32))

        def store(first, second):
            at = 0
            for piece in pieces:
                end = at + piece.shape[0]
                for side, ref in enumerate((first, second)):
                    a, b = max(at, side * half), min(end, (side + 1) * half)
                    if a < b:
                        ref[a - side * half : b - side * half, :] = piece[a - at : b - at]
                at = end

        pl.when(mine_ref[0] == 0)(functools.partial(store, keep_ref, send_ref))
        pl.when(mine_ref[0] == 1)(functools.partial(store, send_ref, keep_ref))


def sum_rows(size):
    return -(-size // 256) * 256


def exchange(x, axis):
    return lax.all_to_all(x, axis, 0, 0)


def halves(n_item):
    return [1 << k for k in range(n_item.bit_length() - 1)]


def reduce_all(x, sizes, beside):
    n_tm, n_item = sizes["tm"], sizes["item"]
    keep, send = x

    def swap(y, by):
        return lax.ppermute(y, "item", [(d, d ^ by) for d in range(n_item)])

    for by in halves(n_item):
        if by > 1:
            half = x.shape[0] // 2
            mine = (lax.axis_index("item") // by) % 2
            keep = lax.dynamic_slice_in_dim(x, mine * half, half)
            send = lax.dynamic_slice_in_dim(x, (1 - mine) * half, half)
        x = keep + swap(send, by)
    if n_item == 1:
        x = jnp.concatenate([keep, send])
    parts = exchange(x.reshape((n_tm, x.shape[0] // n_tm) + x.shape[1:]), "tm")
    x = jnp.sum(parts, axis=0)
    x = exchange(jnp.broadcast_to(x[None], (n_tm,) + x.shape), "tm").reshape((-1,) + x.shape[1:])
    for by in halves(n_item)[::-1]:
        if by == 1:
            x, beside = lax.optimization_barrier((x, beside))
        mine = (lax.axis_index("item") // by) % 2
        other = swap(x, by)
        x = jnp.where(mine == 0, jnp.concatenate([x, other]), jnp.concatenate([other, x]))
    return x, beside


def whole(shape):
    return pl.BlockSpec(shape, lambda i: (0,) * len(shape))


def per_item(shape):
    return pl.BlockSpec((1,) + shape, lambda i: (i,) + (0,) * len(shape))


SMEM = pl.BlockSpec(memory_space=pltpu.SMEM)


def body(
    inputs, lengths, counts, weight_in, bias_in, slope_in, gain_in, shift_in, channelwise_taps, channelwise_bias,
    slope_out, gain_out, shift_out, weight_res, bias_res, weight_skip, bias_skip, grad_residual, grad_skip,
):
    items, frames, base = inputs.shape
    width = weight_in.shape[1]
    sources = grad_skip.shape[1]
    tm, across = lax.axis_size("tm"), lax.axis_size("item")
    place = lax.axis_index("tm").astype(jnp.int32).reshape(1)
    mine = (lax.axis_index("item") % 2).astype(jnp.int32).reshape(1)
    up = [(d, d + 1) for d in range(tm - 1)]
    down = [(d + 1, d) for d in range(tm - 1)]
    x_before = lax.ppermute(inputs[:, frames - TAP :], "tm", up)
    x_after = lax.ppermute(inputs[:, :TAP], "tm", down)

    def row(v):
        return v.reshape(1, -1)

    table = [row(bias_in), row(slope_in), row(gain_in), row(shift_in), channelwise_taps, row(channelwise_bias),
             row(slope_out), row(gain_out), row(shift_out)]
    table_specs = [whole(t.shape) for t in table]
    vmem = lambda mib: pltpu.CompilerParams(vmem_limit_bytes=mib * 2**20)

    rows1, rows2, rows3 = (min(c, frames) for c in (CHUNK1, CHUNK2, CHUNK3))
    v1, st1, ch1 = pl.pallas_call(
        functools.partial(first_kernel, rows1),
        grid=(items,),
        in_specs=[SMEM, SMEM, per_item((frames, base)),
                  pl.BlockSpec((1, rows1, base), lambda i: (jnp.minimum(i + 1, items - 1), 0, 0)),
                  whole((base, width)), whole((1, width)), whole((1, width))],
        out_specs=[per_item((frames, width)), whole((tm, items, LANES)), whole((items, 8, width))],
        out_shape=[jax.ShapeDtypeStruct((items, frames, width), f32), jax.ShapeDtypeStruct((tm, items, LANES), f32),
                   jax.ShapeDtypeStruct((items, 8, width), f32)],
        scratch_shapes=[pltpu.VMEM((3 * base, width), bf16), pltpu.VMEM((2, 8, width), f32)]
        + [pltpu.VMEM((rows1, width), f32)] * 2,
        compiler_params=vmem(58),
        name="first",
    )(lengths, place, inputs, inputs, weight_in, table[0], table[1])
    ga1 = exchange(st1, "tm")

    big = jax.ShapeDtypeStruct((items, frames, width), f32)
    f0, f1, d2, y, ch, st2, bias = pl.pallas_call(
        functools.partial(second_kernel, rows2),
        grid=(items,),
        in_specs=[SMEM, SMEM, SMEM, per_item((frames, width)), per_item((TAP, base)), per_item((TAP, base)),
                  per_item((frames, base)), per_item((sources, frames, base)), whole((base, width)),
                  whole((width, base)), whole((width, base))] + table_specs + [whole((tm, items, LANES))],
        out_specs=[per_item((frames, width))] * 3 + [per_item((2 * base, width)),
                   whole((items, ROWS, width)), whole((tm, items, LANES)), whole((8, 2 * base))],
        out_shape=[big, big, big, jax.ShapeDtypeStruct((items, 2 * base, width), f32), jax.ShapeDtypeStruct((items, ROWS, width), f32),
                   jax.ShapeDtypeStruct((tm, items, LANES), f32), jax.ShapeDtypeStruct((8, 2 * base), f32)],
        scratch_shapes=[pltpu.VMEM((3 * base, width), bf16), pltpu.VMEM((6 * base, width), bf16),
                        pltpu.VMEM((2, items, LANES), f32),
                        pltpu.VMEM((frames + 2 * TAP, width), f32), pltpu.VMEM((ROWS, 8, width), f32),
                        pltpu.VMEM((8, 2 * base), f32), pltpu.VMEM((2 * base, width), f32)]
        + [pltpu.VMEM((rows2, width), f32)] * 2 + [pltpu.VMEM((2, rows2, width), bf16)] * 2
        + [pltpu.VMEM((frames // rows2, 2, rows2, 2 * base), bf16)],
        compiler_params=vmem(48),
        name="second",
    )(lengths, counts, place, v1, x_before, x_after, grad_residual, grad_skip, weight_in, weight_res, weight_skip,
      *table, ga1)
    ga2 = exchange(st2, "tm")

    n_sum = sum_rows(2 * width + 4 * base + 64 + 8)
    out = jax.ShapeDtypeStruct((items, frames, base), f32)
    strip = lambda k: pl.BlockSpec((1, TAP, width), lambda i: (i, k, 0))
    last = frames // TAP - 1
    small = [((5, items, LANES), f32), ((3, items, width), f32), ((16, width), f32), ((items, 2 * base), f32),
             ((base, width), f32), ((8, 8, width), f32)]
    to_last, to_next, *given = pl.pallas_call(
        functools.partial(edge_kernel, frames),
        grid=(items,),
        in_specs=[SMEM, SMEM, per_item((TAP, base)), per_item((TAP, base))] + [strip(0), strip(last)] * 3
        + [whole((items, 8, width)), whole((items, ROWS, width)), whole((base, width)), whole((width, base)),
           whole((width, base))] + table_specs + [whole((tm, items, LANES))] * 2,
        out_specs=[per_item((TAP, base))] * 2 + [whole(shape) for shape, _ in small],
        out_shape=[jax.ShapeDtypeStruct((items, TAP, base), f32)] * 2
        + [jax.ShapeDtypeStruct(shape, dtype) for shape, dtype in small],
        scratch_shapes=[pltpu.VMEM((3 * base, width), bf16), pltpu.VMEM((3 * width, base), bf16)],
        compiler_params=vmem(48),
        name="edge",
    )(lengths, place, x_before, x_after, f0, f0, f1, f1, d2, d2, ch1, ch, weight_in, weight_res, weight_skip, *table,
      ga1, ga2)
    from_next = lax.ppermute(to_last, "tm", down)
    from_last = lax.ppermute(to_next, "tm", up)

    res, skip, gin, *sums = pl.pallas_call(
        functools.partial(third_kernel, rows3),
        grid=(items,),
        in_specs=[SMEM, SMEM, SMEM, per_item((frames, width)), per_item((frames, base)), per_item((frames, width)),
                  per_item((frames, width)), per_item((frames, width)), per_item((frames, base)),
                  per_item((2 * base, width)), whole((items, ROWS, width)),
                  whole((8, 2 * base)), whole((base, width)), whole((width, base)), whole((width, base)),
                  whole((1, base)), whole((1, base))]
        + [whole(shape) for shape, _ in small] + table_specs,
        out_specs=[per_item((frames, base))] * 3 + [whole((n_sum // 2, base))] * 2,
        out_shape=[out, out, out] + [jax.ShapeDtypeStruct((n_sum // 2, base), f32)] * 2,
        scratch_shapes=[pltpu.VMEM((3 * base, width), bf16), pltpu.VMEM((width, 2 * base), bf16),
                        pltpu.VMEM((3 * width, 2 * base), bf16),
                        pltpu.VMEM((frames + 4 * TAP, width), f32),
                        pltpu.VMEM((base, width), f32), pltpu.VMEM((2 * base, width), f32),
                        pltpu.VMEM((8, 8, width), f32)]
        + [pltpu.VMEM((rows3, width), f32)] * 2 + [pltpu.VMEM((2, rows3, width), bf16)] * 2,
        compiler_params=vmem(48),
        cost_estimate=pl.CostEstimate(flops=items * frames * width * base * 30, transcendentals=items * frames * width,
                                      bytes_accessed=items * frames * (5 * width + 7 * base) * 4),
        name="third",
    )(lengths, place, mine, v1, inputs, f0, f1, d2, grad_residual, y, ch, bias, weight_in, weight_res, weight_skip, row(bias_res), row(bias_skip),
      *given, *table)

    sums, from_next, from_last = lax.optimization_barrier((sums, from_next, from_last))
    gin = gin.at[:, frames - TAP :].add(from_next)
    gin = gin.at[:, :TAP].add(from_last)
    total, gin = reduce_all(sums, {"tm": tm, "item": across}, gin)

    g_res, g_skip = total[0:width], total[width : 2 * width]
    at0 = 2 * width + 4 * base
    g_in = total[2 * width : at0].reshape(4, base, LANES).transpose(1, 0, 2).reshape(base, width)
    vec = total[at0 : at0 + 64].reshape(4, 16, LANES).transpose(1, 0, 2).reshape(16, width)
    return (
        res, skip, gin, g_in, vec[0], vec[1], vec[2], vec[3], vec[4:7], vec[7], vec[8], vec[9], vec[10],
        g_res, total[at0 + 64], g_skip, total[at0 + 65],
    )


def solution(mesh):
    spread = P("item", "tm", None)
    return jax.shard_map(
        body,
        mesh=mesh,
        in_specs=(spread, P("item"), P("item")) + (P(),) * 14 + (spread, P("item", None, "tm", None)),
        out_specs=(spread,) * 3 + (P(),) * 14,
        check_vma=False,
    )
```
